256 devices in a mesh: dp: 256 (over y, z, x, core).
Axes of the slice: x: 4, y: 4, z: 8, core: 2. Of those that a mesh axis runs over, the one named last changes fastest.
Arguments:
- features: bfloat16 [256, 1024, 1280], P('dp'), may hold values from -24 to 24
- renoise: bfloat16 [256, 1024, 1280], P('dp'), may hold values from -6 to 6
- critic_grad: bfloat16 [256, 1024, 1280], P('dp'), may hold values from -24 to 24
- student_step: int32 [256], P('dp'), may hold values from 0 to 3
- teacher_step: int32 [256], P('dp'), may hold values from 20 to 979
- student_in: bfloat16 [1280, 640], P('dp'), may hold values from -0.15625 to 0.15625
- student_gain: bfloat16 [1280], P('dp'), may hold values from 0.25 to 1.75
- student_shift: bfloat16 [1280], P('dp'), may hold values from -3 to 3
- student_out: bfloat16 [640, 1280], P(None, 'dp'), may hold values from -0.25 to 0.25
- teacher_in: bfloat16 [1280, 640], P('dp'), may hold values from -0.15625 to 0.15625
- teacher_gain: bfloat16 [1280], P('dp'), may hold values from 0.25 to 1.75
- teacher_shift: bfloat16 [1280], P('dp'), may hold values from -3 to 3
- teacher_out: bfloat16 [640, 1280], P(None, 'dp'), may hold values from -0.25 to 0.25
Outputs:
- grad_in: float32 [1280, 640], P('dp')
- grad_out: float32 [640, 1280], P(None, 'dp')
- grad_gain: float32 [1280], P('dp')
- grad_shift: float32 [1280], P('dp')
The draws below stay inside these ranges and needn't reach their ends.
All inputs are finite; a program needn't handle non-finite values.
Results may differ from the reference program's by a relative error of at most 0.0014.
Values may be sent and summed in bfloat16 or wider, within the bound.
A program may use at most 128 MiB of HBM per device.

```python
import math
import jax
import jax.numpy as jnp
from jax import lax

C = 1280
H = 640
P_SIZE = 1024
GROUPS = 32
STEPS_T = 1000
LATENTS = 256


def place_ends(values, key, low, high):
    place = [jax.random.randint(jax.random.fold_in(key, axis), (), 0, length) for axis, length in enumerate(values.shape)]
    widest = values.shape.index(max(values.shape))
    next_to = place[:widest] + [(place[widest] + 1) % values.shape[widest]] + place[widest + 1:]
    return values.at[tuple(place)].set(low).at[tuple(next_to)].set(high)


def spiked(entries, rng, source, target, shards_of, factor):
    def block_of(position):
        return (jnp.arange(entries.shape[position]) // (entries.shape[position] // shards_of)).reshape((-1,) + (1,) * (entries.ndim - 1 - position))

    one_side = jax.random.permutation(rng, shards_of)[block_of(target)]
    other_side = (block_of(target) + shards_of // 2) % shards_of
    return jnp.where((block_of(source) == one_side) | (block_of(source) == other_side), factor * entries, entries)


def level_of(stream_key, shape, cuts, least, largest):
    level = 1.0
    for dim, shards_of in cuts:
        heights = jax.random.uniform(jax.random.fold_in(jax.random.fold_in(stream_key, 6), dim), (shards_of,), jnp.float32, least / len(cuts), largest / len(cuts))
        level = level * jnp.repeat(jnp.exp(heights), shape[dim] // shards_of).reshape((-1,) + (1,) * (len(shape) - 1 - dim))
    return level


def centred(rng, shape, scale, limit, cuts=(), held_as=jnp.bfloat16):
    level = level_of(rng, shape, cuts, -0.22, 0.18) if cuts else 1.0
    values = jax.random.normal(rng, shape, jnp.float32) * scale * level
    return jnp.minimum(jnp.maximum(values, -limit), limit).astype(held_as)


def noise_with(own_key, dims, scale, bound, cuts, heavy, kind=jnp.bfloat16):
    result = scale * jax.random.normal(own_key, dims, jnp.float32)
    if cuts:
        result = result * level_of(own_key, dims, cuts, -0.22, 0.18)
    return jnp.clip(spiked(result, jax.random.fold_in(own_key, 3), *heavy), -bound, bound).astype(kind)


def setup_inputs(seed: int = 0) -> dict:
    seeds = jax.random.split(jax.random.key(seed), 14)
    return {
        "features": noise_with(seeds[0], (LATENTS, P_SIZE, C), 1.0, 24.0, ((0, 256),), (0, 2, 256, 6.0)),
        "renoise": centred(seeds[1], (LATENTS, P_SIZE, C), 1.0, 6.0, ((0, 256),)),
        "critic_grad": noise_with(seeds[2], (LATENTS, P_SIZE, C), 1.0, 24.0, ((0, 256),), (0, 2, 256, 6.0)),
        "student_step": place_ends(jax.random.randint(seeds[3], (LATENTS,), 0, 4), jax.random.fold_in(seeds[3], 1), 0, 3).astype(jnp.int32),
        "teacher_step": place_ends(jax.random.randint(seeds[4], (LATENTS,), 20, 980), jax.random.fold_in(seeds[4], 1), 20, 979).astype(jnp.int32),
        "student_in": centred(seeds[5], (C, H), C ** -0.5, 0.15625, ((0, 256),)),
        "student_gain": jnp.clip(1.0 + 0.15 * jax.random.normal(seeds[6], (C,), jnp.float32), 0.25, 1.75).astype(jnp.bfloat16),
        "student_shift": centred(seeds[7], (C,), 0.5, 3.0, ((0, 256),)),
        "student_out": centred(seeds[8], (H, C), H ** -0.5, 0.25, ((1, 256),)),
        "teacher_in": centred(seeds[9], (C, H), C ** -0.5, 0.15625, ((0, 256),)),
        "teacher_gain": jnp.clip(1.0 + 0.15 * jax.random.normal(seeds[10], (C,), jnp.float32), 0.25, 1.75).astype(jnp.bfloat16),
        "teacher_shift": centred(seeds[11], (C,), 0.5, 3.0, ((0, 256),)),
        "teacher_out": centred(seeds[12], (H, C), H ** -0.5, 0.25, ((1, 256),)),
    }


EPS = 1e-05

def plan():
    steps = jnp.arange(STEPS_T).astype(jnp.float32)
    lo = math.sqrt(0.00085)
    hi = math.sqrt(0.012)
    betas = (lo + (hi - lo) * steps / (STEPS_T - 1)) ** 2
    return jnp.exp(jnp.cumsum(jnp.log(1.0 - betas)))

def embed(tvals):
    half = H // 2
    freqs = jnp.exp(-math.log(10000.0) * jnp.arange(half).astype(jnp.float32) / half)
    angles = tvals[:, None] * freqs[None, :]
    return jnp.concatenate([jnp.cos(angles), jnp.sin(angles)], axis=1)

def group_norm(field):
    batch, rows, chans = field.shape
    width = chans // GROUPS
    count = rows * width
    mean_g = lax.optimization_barrier(jnp.sum(lax.optimization_barrier(jnp.sum(field, axis=1)).reshape(batch, GROUPS, width), axis=2)) / count
    centered = field - jnp.repeat(mean_g, width, axis=1)[:, None, :]
    var_g = lax.optimization_barrier(jnp.sum(lax.optimization_barrier(jnp.sum(centered * centered, axis=1)).reshape(batch, GROUPS, width), axis=2)) / count
    return centered * jnp.repeat(lax.rsqrt(var_g + EPS), width, axis=1)[:, None, :]

def block(field, w_in, gain, shift, w_out, emb):
    batch, rows, chans = field.shape
    normed = group_norm(field)
    hid = (normed * gain.astype(jnp.float32) + shift.astype(jnp.float32)).astype(jnp.bfloat16)
    pre = jnp.dot(hid.reshape(batch * rows, chans), w_in, preferred_element_type=jnp.float32)
    pre = pre.reshape(batch, rows, -1) + emb[:, None, :]
    act = jax.nn.silu(pre).astype(jnp.bfloat16)
    proj = jnp.dot(act.reshape(batch * rows, -1), w_out, preferred_element_type=jnp.float32)
    return (normed, hid, pre, act, field + proj.reshape(batch, rows, chans))

def reference(features, renoise, critic_grad, student_step, teacher_step, student_in, student_gain, student_shift, student_out, teacher_in, teacher_gain, teacher_shift, teacher_out):
    keep_table = plan()
    norm = 1.0 / math.sqrt(P_SIZE * LATENTS)

    def one(carry, item):
        acc_in, acc_out, acc_gain, acc_shift = carry
        feat, noise, critic, sstep, tstep = item
        field = feat.astype(jnp.float32)[None]
        tval_s = (999 - 250 * sstep).astype(jnp.float32).reshape(1)
        normed, hid, pre, act, sample = block(field, student_in, student_gain, student_shift, student_out, embed(tval_s))
        keep = jnp.sum(jnp.where(jnp.arange(STEPS_T) == tstep, keep_table, 0.0))
        noisy = (jnp.sqrt(keep) * sample + jnp.sqrt(1.0 - keep) * noise.astype(jnp.float32)[None]).astype(jnp.bfloat16)
        tval_t = tstep.astype(jnp.float32).reshape(1)
        target = block(noisy.astype(jnp.float32), teacher_in, teacher_gain, teacher_shift, teacher_out, embed(tval_t))[4]
        d_sample = ((2.0 * keep * (sample - target) + critic.astype(jnp.float32)[None]) * norm).astype(jnp.bfloat16)
        ds2 = d_sample.reshape(P_SIZE, C)
        act2 = act.reshape(P_SIZE, H)
        hid2 = hid.reshape(P_SIZE, C)
        acc_out = acc_out + jnp.dot(act2.T, ds2, preferred_element_type=jnp.float32)
        d_act = lax.dot_general(ds2, student_out, (((1,), (1,)), ((), ())), preferred_element_type=jnp.float32)
        sig = jax.nn.sigmoid(pre.reshape(P_SIZE, H))
        d_pre = (d_act * sig * (1.0 + pre.reshape(P_SIZE, H) * (1.0 - sig))).astype(jnp.bfloat16)
        acc_in = acc_in + jnp.dot(hid2.T, d_pre, preferred_element_type=jnp.float32)
        d_hid = lax.dot_general(d_pre, student_in, (((1,), (1,)), ((), ())), preferred_element_type=jnp.float32)
        acc_gain = acc_gain + lax.optimization_barrier(jnp.sum(d_hid * normed.reshape(P_SIZE, C), axis=0))
        acc_shift = acc_shift + lax.optimization_barrier(jnp.sum(d_hid, axis=0))
        return ((acc_in, acc_out, acc_gain, acc_shift), None)
    init = (jnp.zeros((C, H), jnp.float32), jnp.zeros((H, C), jnp.float32), jnp.zeros((C,), jnp.float32), jnp.zeros((C,), jnp.float32))
    sums, unused = lax.scan(one, init, (features, renoise, critic_grad, student_step, teacher_step))
    return (sums[0], sums[1], sums[2], sums[3])
```

```python
import functools
import math

import jax
import jax.numpy as jnp
import numpy as np
from jax import lax
from jax.experimental import pallas as pl
from jax.experimental.pallas import tpu as pltpu
from jax.sharding import PartitionSpec as P

GROUPS = 32
STEPS_T = 1000
EPS = 1e-05
MESH = pl.DeviceIdType.MESH
F32 = jnp.float32
BF16 = jnp.bfloat16


def keep_of(step):
    steps = jnp.arange(STEPS_T).astype(F32)
    lo = math.sqrt(0.00085)
    hi = math.sqrt(0.012)
    betas = (lo + (hi - lo) * steps / (STEPS_T - 1)) ** 2
    logs = jnp.log(1.0 - betas)
    return jnp.exp(jnp.sum(jnp.where(jnp.arange(STEPS_T) <= step, logs, 0.0)))


def embed(tval, width):
    half = width // 2
    freqs = jnp.exp(-math.log(10000.0) * jnp.arange(half).astype(F32) / half)
    angles = tval * freqs
    return jnp.concatenate([jnp.cos(angles), jnp.sin(angles)])[None, :]


def dev(y, z, x, c):
    return ((y * 8 + z) * 4 + x) * 2 + c


def where_am_i():
    me = lax.axis_index("dp")
    c = lax.rem(me, 2)
    x = lax.rem(lax.div(me, 2), 4)
    z = lax.rem(lax.div(me, 8), 8)
    y = lax.div(me, 64)
    return y, z, x, c


class Ring:
    def __init__(self, b, y, z, x, c):
        r = lax.rem(c + b, 2)
        self.r = r
        self.p = (1 - r) * y + r * x
        self.q = (1 - r) * x + r * y
        self.at = (y, z, x, c)

    def block(self, dp, dq):
        pp = lax.rem(self.p + dp, 4)
        qq = lax.rem(self.q + dq, 4)
        return pp * (4 - 3 * self.r) + qq * (1 + 3 * self.r)

    def first(self, d):
        y, z, x, c = self.at
        r = self.r
        return dev(lax.rem(y + (1 - r) * d, 4), z, lax.rem(x + r * d, 4), c)

    def second(self, d):
        y, z, x, c = self.at
        r = self.r
        return dev(lax.rem(y + r * d, 4), z, lax.rem(x + (1 - r) * d, 4), c)


def signal(device):
    pl.semaphore_signal(pltpu.get_barrier_semaphore(), inc=1, device_id=(device,), device_id_type=MESH)


def remote(src, dst, ssem, rsem, device):
    return pltpu.make_async_remote_copy(
        src_ref=src, dst_ref=dst, send_sem=ssem, recv_sem=rsem, device_id=(device,), device_id_type=MESH
    )


def greet_planes(y, z, x, c):
    for d in (1, 3):
        signal(dev(y, z, lax.rem(x + d, 4), c))
        signal(dev(lax.rem(y + d, 4), z, x, c))
    signal(dev(y, z, x, 1 - c))


def gather_kernel(raw_ref, sel_ref, w_ref, vec_ref, rbuf, wb, r_send, r_recv, s_send, s_recv, s_sib):
    y, z, x, c = where_am_i()
    mine = lax.div(z, 2) == x
    greet_planes(y, z, x, c)
    for k in range(1, 16):
        signal(dev(y, 2 * x + lax.rem(z + k // 8, 2), lax.rem(x + k // 2, 4), lax.rem(c + k, 2)))

    @pl.when(jnp.logical_not(mine))
    def _():
        signal(dev(y, 2 * x + lax.rem(z, 2), x, c))

    pl.semaphore_wait(pltpu.get_barrier_semaphore(), jnp.where(mine, 20, 21))

    slot = lax.rem(z, 2) * 8 + x * 2 + c
    to_x = lax.div(z, 2)
    own = pltpu.make_async_copy(raw_ref.at[c], rbuf.at[slot], r_recv)
    for k in range(1, 16):
        cc = lax.rem(c + k, 2)
        remote(
            raw_ref.at[cc], rbuf.at[slot], r_send, r_recv, dev(y, lax.rem(z + k // 2, 8), to_x, cc)
        ).start()
    first = remote(raw_ref.at[c], rbuf.at[slot], r_send, r_recv, dev(y, z, to_x, c))

    @pl.when(mine)
    def _():
        own.start()

    @pl.when(jnp.logical_not(mine))
    def _():
        first.start()

    pltpu.make_async_copy(rbuf, rbuf, r_recv).wait()

    rings = [Ring(b, y, z, x, c) for b in range(2)]

    def at(b, g, core=None):
        return wb.at[(b * 2 + (c if core is None else core)) * 16 + g]

    def send(b, g, device):
        remote(at(b, g), at(b, g), s_send.at[b], s_recv.at[b, g], device).start()

    def to_sibling(b, g):
        remote(at(b, g), at(b, g), s_send.at[b], s_sib.at[b], dev(y, z, x, 1 - c)).start()

    def wait(b, g):
        remote(at(b, g), at(b, g), s_send.at[b], s_recv.at[b, g], dev(y, z, x, 1 - c)).wait_recv()

    row = lax.broadcasted_iota(jnp.int32, (16, 128), 0)
    for b in range(2):
        ring = rings[b]
        g = ring.block(0, 0)
        k = (b * 2 + c) * 16 + g
        outs = []
        for h in range(2):
            t = 2 * b + h
            raw = rbuf[:, 16 * t : 16 * t + 16, :].reshape(256, 128)
            out = jnp.dot(sel_ref[...], raw, preferred_element_type=F32)
            outs.append(out[240:256])
            for i in range(3):
                j = 3 * h + i
                if j < 5:
                    wb[k, 80 * j : 80 * j + 80, :] = out[80 * i : 80 * i + 80].astype(BF16)
        wb[k, 400:416, :] = jnp.where(row == 0, outs[0], outs[1]).astype(BF16)
        send(b, g, ring.first(1))
        send(b, g, ring.first(3))
        send(b, g, ring.second(1))
        send(b, g, ring.second(3))
        to_sibling(b, g)

    for b in range(2):
        ring = rings[b]
        for d in (3, 1, 2):
            g = ring.block(d, 0)
            wait(b, g)
            if d == (3 if b == 0 else 1):
                send(b, g, ring.first(1 if b == 0 else 3))
            send(b, g, ring.second(1))
            send(b, g, ring.second(3))
            to_sibling(b, g)
        for n, d in enumerate((0, 3, 1, 2)):
            for e in (3, 1):
                g = ring.block(d, e)
                wait(b, g)
                if e == (3 if n % 2 == 0 else 1):
                    send(b, g, ring.second(1 if e == 3 else 3))
                to_sibling(b, g)
        for d in (0, 3, 1, 2):
            g = ring.block(d, 2)
            wait(b, g)
            to_sibling(b, g)

    for b in range(2):
        pltpu.make_async_copy(wb.at[pl.ds(0, 16)], wb.at[pl.ds(0, 16)], s_sib.at[b]).wait()
    for b in range(2):
        pltpu.make_async_copy(wb.at[pl.ds(0, 31)], wb.at[pl.ds(0, 31)], s_send.at[b]).wait()
    @pl.when(mine)
    def _():
        pltpu.make_async_copy(rbuf.at[pl.ds(0, 15)], rbuf.at[pl.ds(0, 15)], r_send).wait()

    @pl.when(jnp.logical_not(mine))
    def _():
        pltpu.make_async_copy(rbuf, rbuf, r_send).wait()

    for n in range(4):
        for j in range(5):
            w_ref[n, :, 128 * j : 128 * j + 128] = wb[16 * n : 16 * n + 16, 80 * j : 80 * j + 80, :].reshape(1280, 128)
    lane = lax.broadcasted_iota(jnp.int32, (16, 128), 1)
    for b in range(2):
        acc = [jnp.zeros((16, 128), F32) for _ in range(10)]
        for g in range(16):
            block, s = divmod(80 * g, 128)
            v = wb[2 * b * 16 + g, 400:416, :].astype(F32)
            if s:
                v = pltpu.roll(v, s, 1)
            acc[block] += jnp.where(lane >= s, v, 0.0)
            if s + 80 > 128:
                acc[block + 1] += jnp.where(lane < s, v, 0.0)
        for n in range(10):
            vec_ref[b, :, 128 * n : 128 * n + 128] = acc[n]


def selection():
    sel = np.zeros((256, 256), np.float32)
    for m in range(240):
        i, q = divmod(m, 80)
        sel[m, 16 * (q // 5) + 5 * i + q % 5] = 1.0
    for d in range(16):
        sel[240:242, 16 * d + 15] = 1.0
    return jnp.asarray(sel, BF16)


def packed(student, teacher, vectors):
    tiles = []
    for shard, (gain, shift) in ((student, vectors[0]), (teacher, vectors[1])):
        slabs = shard.reshape(5, 5, 128).transpose(1, 0, 2).reshape(25, 128)
        tiles += [slabs[:15], gain, slabs[15:], jnp.zeros((5, 128), BF16), shift]
    return jnp.concatenate(tiles)


def gather(student_in, student_gain, student_shift, student_out, teacher_in, teacher_gain, teacher_shift, teacher_out):
    place = 5 * lax.rem(lax.axis_index("dp"), 16)

    def spread(v):
        return lax.dynamic_update_slice(jnp.zeros((1, 128), BF16), v[None, :], (0, place))

    vectors = ((spread(student_gain), spread(student_shift)), (spread(teacher_gain), spread(teacher_shift)))
    raw = jnp.stack([packed(student_in, teacher_in, vectors), packed(student_out.T, teacher_out.T, vectors)])
    vmem = pl.BlockSpec(memory_space=pltpu.VMEM)
    return pl.pallas_call(
        gather_kernel,
        out_shape=(jax.ShapeDtypeStruct((4, 1280, 640), BF16), jax.ShapeDtypeStruct((2, 16, 1280), F32)),
        in_specs=[vmem, vmem],
        out_specs=(vmem, vmem),
        scratch_shapes=[
            pltpu.VMEM((16, 64, 128), BF16),
            pltpu.VMEM((64, 416, 128), BF16),
            pltpu.SemaphoreType.DMA,
            pltpu.SemaphoreType.DMA,
            pltpu.SemaphoreType.DMA((2,)),
            pltpu.SemaphoreType.DMA((2, 16)),
            pltpu.SemaphoreType.DMA((2,)),
        ],
        compiler_params=pltpu.CompilerParams(collective_id=0, has_side_effects=True, vmem_limit_bytes=48 * 2**20),
    )(raw, selection())


def scatter_kernel(
    g_ref, o_ref, sib, t1, fm, fp, acc, u1, um, up, stage, fin,
    h_send, h_recv, q_send, t_recv, m_recv, p_recv, p_send, ut_recv, um_recv, up_recv, f_send, f_recv,
):
    y, z, x, c = where_am_i()
    selfish = (2 * x + c) == z
    greet_planes(y, z, x, c)
    from_x, from_c = lax.div(z, 2), lax.rem(z, 2)
    for k in range(1, 8):
        signal(dev(y, lax.rem(z + k, 8), from_x, from_c))

    @pl.when(jnp.logical_not(selfish))
    def _():
        signal(dev(y, z, from_x, from_c))

    pl.semaphore_wait(pltpu.get_barrier_semaphore(), jnp.where(selfish, 12, 13))

    rings = [Ring(b, y, z, x, c) for b in range(2)]
    order = [(d, 2) for d in (2, 1, 3, 0)] + [(d, e) for d in (2, 1, 3, 0) for e in (1, 3)] + [(d, 0) for d in (2, 1, 3, 0)]

    def to_sibling(b, g):
        return remote(g_ref.at[b, g, 1 - c], sib.at[b, g], h_send.at[b], h_recv.at[b, g], dev(y, z, x, 1 - c))

    for b in range(2):
        other = Ring(b + 1, y, z, x, c)
        for d, e in order:
            to_sibling(b, other.block(d, e)).start()

    def meet(b, g):
        to_sibling(b, g).wait_recv()
        sib[b, g] += g_ref[b, g, c]

    for b in range(2):
        ring = rings[b]

        def push(g, dst, recv, d):
            remote(sib.at[b, g], dst, q_send.at[b], recv, ring.second(d)).start()

        for k in range(4):
            d = (2, 1, 3, 0)[k]
            g = ring.block(d, 2)
            meet(b, g)
            push(g, t1.at[b, k], t_recv.at[b, k], 1 if k % 2 == 0 else 3)
        for k in range(4):
            d = (2, 1, 3, 0)[k]
            for e in (3, 1) if k % 2 == 0 else (1, 3):
                g = ring.block(d, e)
                meet(b, g)
                if e == (1 if k % 2 == 0 else 3):
                    remote(t1.at[b, k], t1.at[b, k], q_send.at[b], t_recv.at[b, k], ring.second(1)).wait_recv()
                    sib[b, g] += t1[b, k]
                if e == 1:
                    push(g, fm.at[b, k], m_recv.at[b, k], 1)
                else:
                    push(g, fp.at[b, k], p_recv.at[b, k], 3)

    for b in range(2):
        ring = rings[b]

        def push1(k, dst, recv, d):
            remote(acc.at[b, k], dst, p_send.at[b], recv, ring.first(d)).start()

        def arrive(dst, recv):
            remote(dst, dst, p_send.at[b], recv, ring.first(1)).wait_recv()

        for k in range(4):
            d = (2, 1, 3, 0)[k] if b == 0 else (2, 3, 1, 0)[k]
            kk = (2, 1, 3, 0).index(d)
            g = ring.block(d, 0)
            meet(b, g)
            arrive(fm.at[b, kk], m_recv.at[b, kk])
            arrive(fp.at[b, kk], p_recv.at[b, kk])
            acc[b, k] = sib[b, g] + fm[b, kk] + fp[b, kk]
            if k == 0:
                push1(k, u1.at[b], ut_recv.at[b], 1 if b == 0 else 3)
            if k == 1:
                arrive(u1.at[b], ut_recv.at[b])
                acc[b, k] += u1[b]
            if k in (1, 2):
                if d == 1:
                    push1(k, um.at[b], um_recv.at[b], 1)
                else:
                    push1(k, up.at[b], up_recv.at[b], 3)
        arrive(um.at[b], um_recv.at[b])
        arrive(up.at[b], up_recv.at[b])
        total = acc[b, 3] + um[b] + up[b]
        for s in range(8):
            for j in range(5):
                stage[b, s, 0:5, 128 * j : 128 * j + 128] = total[40 * j + 5 * s : 40 * j + 5 * s + 5]
            v = total[200:208]
            if s:
                v = pltpu.roll(v, 128 - 5 * s, 1)
            stage[b, s, 5:7, 0:128] = v[0:2]
        for k in range(1, 8):
            s = lax.rem(x * 2 + c + k, 8)
            remote(
                stage.at[b, s], fin.at[b, z], f_send.at[b], f_recv.at[b],
                dev(y, 2 * x + c, lax.div(s, 2), lax.rem(s, 2)),
            ).start()
        s = x * 2 + c
        own = pltpu.make_async_copy(stage.at[b, s], fin.at[b, z], f_recv.at[b])
        far = remote(stage.at[b, s], fin.at[b, z], f_send.at[b], f_recv.at[b], dev(y, 2 * x + c, x, c))

        @pl.when(selfish)
        def _():
            own.start()

        @pl.when(jnp.logical_not(selfish))
        def _():
            far.start()

    for b in range(2):
        pltpu.make_async_copy(fin.at[b], fin.at[b], f_recv.at[b]).wait()
        o_ref[b] = jnp.sum(fin[b], axis=0)
    for b in range(2):
        pltpu.make_async_copy(sib.at[b], sib.at[b], h_send.at[b]).wait()
        pltpu.make_async_copy(sib.at[b, pl.ds(0, 12)], sib.at[b, pl.ds(0, 12)], q_send.at[b]).wait()
        pltpu.make_async_copy(acc.at[b, pl.ds(0, 3)], acc.at[b, pl.ds(0, 3)], p_send.at[b]).wait()

        @pl.when(selfish)
        def _():
            pltpu.make_async_copy(fin.at[b, pl.ds(0, 7)], fin.at[b, pl.ds(0, 7)], f_send.at[b]).wait()

        @pl.when(jnp.logical_not(selfish))
        def _():
            pltpu.make_async_copy(fin.at[b], fin.at[b], f_send.at[b]).wait()


def scatter(grads):
    vmem = pl.BlockSpec(memory_space=pltpu.VMEM)
    block = (208, 128)
    dma = pltpu.SemaphoreType.DMA
    return pl.pallas_call(
        scatter_kernel,
        out_shape=jax.ShapeDtypeStruct((2, 8, 640), F32),
        in_specs=[vmem],
        out_specs=vmem,
        scratch_shapes=[
            pltpu.VMEM((2, 16, *block), F32),
            pltpu.VMEM((2, 4, *block), F32),
            pltpu.VMEM((2, 4, *block), F32),
            pltpu.VMEM((2, 4, *block), F32),
            pltpu.VMEM((2, 4, *block), F32),
            pltpu.VMEM((2, *block), F32),
            pltpu.VMEM((2, *block), F32),
            pltpu.VMEM((2, *block), F32),
            pltpu.VMEM((2, 8, 8, 640), F32),
            pltpu.VMEM((2, 8, 8, 640), F32),
            dma((2,)),
            dma((2, 16)),
            dma((2,)),
            dma((2, 4)),
            dma((2, 4)),
            dma((2, 4)),
            dma((2,)),
            dma((2,)),
            dma((2,)),
            dma((2,)),
            dma((2,)),
            dma((2,)),
        ],
        compiler_params=pltpu.CompilerParams(collective_id=1, has_side_effects=True, vmem_limit_bytes=48 * 2**20),
    )(grads)


def group_norm(field):
    rows, chans = field.shape
    width = chans // GROUPS
    count = rows * width
    mean_g = jnp.sum(jnp.sum(field, axis=0).reshape(GROUPS, width), axis=1) / count
    centered = field - jnp.repeat(mean_g, width)[None, :]
    var_g = jnp.sum(jnp.sum(centered * centered, axis=0).reshape(GROUPS, width), axis=1) / count
    return centered * jnp.repeat(lax.rsqrt(var_g + EPS), width)[None, :]


def block(field, w_in, gain, shift, w_out_t, emb):
    normed = group_norm(field)
    hid = (normed * gain + shift).astype(BF16)
    pre = jnp.dot(hid, w_in, preferred_element_type=F32) + emb
    act = jax.nn.silu(pre).astype(BF16)
    proj = lax.dot_general(act, w_out_t, (((1,), (1,)), ((), ())), preferred_element_type=F32)
    return normed, hid, pre, act, field + proj


def local(
    features,
    renoise,
    critic_grad,
    student_step,
    teacher_step,
    student_in,
    student_gain,
    student_shift,
    student_out,
    teacher_in,
    teacher_gain,
    teacher_shift,
    teacher_out,
):
    rows, chans = features.shape[1:]
    inner = student_in.shape[1]
    norm = 1.0 / math.sqrt(rows * lax.axis_size("dp"))
    w, vec = gather(
        student_in, student_gain, student_shift, student_out, teacher_in, teacher_gain, teacher_shift, teacher_out
    )
    field = features[0].astype(F32)
    tval_s = (999 - 250 * student_step[0]).astype(F32)
    normed, hid, pre, act, sample = block(field, w[0], vec[0, 0:1], vec[0, 1:2], w[1], embed(tval_s, inner))
    keep = keep_of(teacher_step[0])
    noisy = (jnp.sqrt(keep) * sample + jnp.sqrt(1.0 - keep) * renoise[0].astype(F32)).astype(BF16)
    target = block(
        noisy.astype(F32), w[2], vec[1, 0:1], vec[1, 1:2], w[3], embed(teacher_step[0].astype(F32), inner)
    )[4]
    d_sample = ((2.0 * keep * (sample - target) + critic_grad[0].astype(F32)) * norm).astype(BF16)
    rows_of = (((0,), (0,)), ((), ()))
    term_out = lax.dot_general(d_sample, act, rows_of, preferred_element_type=F32)
    d_act = jnp.dot(d_sample, w[1], preferred_element_type=F32)
    sig = jax.nn.sigmoid(pre)
    d_pre = (d_act * sig * (1.0 + pre * (1.0 - sig))).astype(BF16)
    term_in = lax.dot_general(hid, d_pre, rows_of, preferred_element_type=F32)
    d_hid = lax.dot_general(d_pre, w[0], (((1,), (1,)), ((), ())), preferred_element_type=F32)
    vecs = jnp.stack([jnp.sum(d_hid * normed, axis=0), jnp.sum(d_hid, axis=0)])
    vecs = jnp.pad(vecs.reshape(2, 32, 40).transpose(1, 0, 2), ((0, 0), (0, 6), (0, 88)))
    slabs = jnp.stack([term_out, term_in]).reshape(2, 32, 40, 5, 128).transpose(0, 1, 3, 2, 4).reshape(2, 32, 200, 128)
    grads = jnp.concatenate([slabs, jnp.broadcast_to(vecs, (2, 32, 8, 128))], axis=2).reshape(2, 16, 2, 208, 128)
    out = scatter(grads)
    return out[1, :5], out[0, :5].T, out[1, 5, :5], out[1, 6, :5]


def solution(mesh):
    return jax.shard_map(
        local,
        mesh=mesh,
        in_specs=(
            P("dp", None, None),
            P("dp", None, None),
            P("dp", None, None),
            P("dp"),
            P("dp"),
            P("dp", None),
            P("dp"),
            P("dp"),
            P(None, "dp"),
            P("dp", None),
            P("dp"),
            P("dp"),
            P(None, "dp"),
        ),
        out_specs=(P("dp", None), P(None, "dp"), P("dp"), P("dp")),
        check_vma=False,
    )
```

```python
import functools
import math

import jax
import jax.numpy as jnp
import numpy as np
from jax import lax
from jax.experimental import pallas as pl
from jax.experimental.pallas import tpu as pltpu
from jax.sharding import PartitionSpec as P

GROUPS = 32
STEPS_T = 1000
EPS = 1e-05
MESH = pl.DeviceIdType.MESH
F32 = jnp.float32
BF16 = jnp.bfloat16


def dev(y, z, x, c):
    return ((y * 8 + z) * 4 + x) * 2 + c


def where_am_i():
    me = lax.axis_index("dp")
    c = lax.rem(me, 2)
    x = lax.rem(lax.div(me, 2), 4)
    z = lax.rem(lax.div(me, 8), 8)
    y = lax.div(me, 64)
    return y, z, x, c


class Ring:
    def __init__(self, b, y, z, x, c):
        r = lax.rem(c + b, 2)
        self.r = r
        self.p = (1 - r) * y + r * x
        self.q = (1 - r) * x + r * y
        self.at = (y, z, x, c)

    def block(self, dp, dq):
        pp = lax.rem(self.p + dp, 4)
        qq = lax.rem(self.q + dq, 4)
        return pp * (4 - 3 * self.r) + qq * (1 + 3 * self.r)

    def first(self, d):
        y, z, x, c = self.at
        r = self.r
        return dev(lax.rem(y + (1 - r) * d, 4), z, lax.rem(x + r * d, 4), c)

    def second(self, d):
        y, z, x, c = self.at
        r = self.r
        return dev(lax.rem(y + r * d, 4), z, lax.rem(x + (1 - r) * d, 4), c)


def signal(device):
    pl.semaphore_signal(pltpu.get_barrier_semaphore(), inc=1, device_id=(device,), device_id_type=MESH)


def remote(src, dst, ssem, rsem, device):
    return pltpu.make_async_remote_copy(
        src_ref=src, dst_ref=dst, send_sem=ssem, recv_sem=rsem, device_id=(device,), device_id_type=MESH
    )


def greet_planes(y, z, x, c):
    for d in (1, 3):
        signal(dev(y, z, lax.rem(x + d, 4), c))
        signal(dev(lax.rem(y + d, 4), z, x, c))
    signal(dev(y, z, x, 1 - c))


ROWS = 256
STEPS = 4


def plan_of(step):
    index = lax.broadcasted_iota(jnp.int32, (8, 128), 0) * 128 + lax.broadcasted_iota(jnp.int32, (8, 128), 1)
    lo = math.sqrt(0.00085)
    hi = math.sqrt(0.012)
    betas = (lo + (hi - lo) * index.astype(F32) / (STEPS_T - 1)) ** 2
    logs = jnp.where(index <= step, jnp.log(1.0 - betas), 0.0)
    return jnp.exp(jnp.sum(jnp.sum(logs, axis=1, keepdims=True), axis=0, keepdims=True))


def embed(tval, width):
    half = width // 2
    lane = lax.broadcasted_iota(jnp.int32, (8, width), 1)
    index = jnp.where(lane < half, lane, lane - half).astype(F32)
    angles = tval * jnp.exp(-math.log(10000.0) * index / half)
    return jnp.where(lane < half, jnp.cos(angles), jnp.sin(angles))


def by_parts(value, indicator, dims):
    total = None
    for _ in range(3):
        part = value.astype(BF16)
        value = value - part.astype(F32)
        term = lax.dot_general(part, indicator, (dims, ((), ())), preferred_element_type=F32)
        total = term if total is None else total + term
    return total


def per_group(sums, indicator, count):
    groups = by_parts(sums, indicator, ((1,), (0,)))
    return jnp.broadcast_to(jnp.sum(groups, axis=0, keepdims=True), groups.shape) / count


def per_channel(groups, indicator):
    return by_parts(groups, indicator, ((1,), (1,)))


def eights(value):
    return jnp.sum(value.reshape(value.shape[0] // 8, 8, value.shape[1]), axis=0)


def kernel(
    feat_hbm, noise_hbm, critic_hbm, s_step, t_step, si_ref, so_ref, ti_ref, to_ref, vecs_ref, sel_ref, ind_ref,
    o_ref,
    feat, noise, critic, rawf, raw, rbuf, wb, w, vec, hid, pre, act, sample, dpre, sums, stat, emb,
    grad, sib, t1, fm, fp, acc, u1, um, up, stage, fin,
    l_sem, r_send, r_recv, s_send, s_recv, s_sib,
    h_send, h_recv, q_send, t_recv, m_recv, p_recv, p_send, ut_recv, um_recv, up_recv, f_send, f_recv,
):
    y, z, x, c = where_am_i()
    mine = lax.div(z, 2) == x
    selfish = (2 * x + c) == z
    loads = [
        pltpu.make_async_copy(src.at[0], dst, l_sem.at[n])
        for n, (src, dst) in enumerate(((feat_hbm, feat), (noise_hbm, noise), (critic_hbm, critic)))
    ]
    loads[0].start()

    greet_planes(y, z, x, c)
    for k in range(1, 16):
        signal(dev(y, 2 * x + lax.rem(z + k // 8, 2), lax.rem(x + k // 2, 4), lax.rem(c + k, 2)))

    @pl.when(jnp.logical_not(mine))
    def _():
        signal(dev(y, 2 * x + lax.rem(z, 2), x, c))

    for k in range(1, 8):
        signal(dev(y, lax.rem(z + k, 8), lax.div(z, 2), lax.rem(z, 2)))

    @pl.when(jnp.logical_not(selfish))
    def _():
        signal(dev(y, z, lax.div(z, 2), lax.rem(z, 2)))

    rawf[...] = jnp.zeros_like(rawf)
    place = 5 * lax.rem(lax.axis_index("dp"), 16)
    spread = pltpu.roll(vecs_ref[...], place, 1)
    for core, pair in enumerate(((si_ref, ti_ref), (so_ref, to_ref))):
        for b, ref in enumerate(pair):
            shard = ref[...].astype(F32)
            for j in range(5):
                r = 16 * (2 * b + j // 3) + 5 * (j % 3)
                rawf[core, r : r + 5, :] = shard[:, 128 * j : 128 * j + 128]
            for h in range(2):
                r = 16 * (2 * b + h) + 15
                rawf[core, r : r + 1, :] = spread[2 * b + h : 2 * b + h + 1]
    raw[...] = rawf[...].astype(BF16)
    loads[0].wait()
    loads[1].start()
    loads[2].start()

    def rows_of(i):
        return pl.ds(pl.multiple_of(i * ROWS, ROWS), ROWS)

    sums[...] = jnp.zeros_like(sums)

    @pl.loop(0, STEPS)
    def _(i):
        sums[0] += eights(feat[rows_of(i), :].astype(F32))

    pl.semaphore_wait(pltpu.get_barrier_semaphore(), jnp.where(mine, 20, 21) + jnp.where(selfish, 7, 8))

    slot = lax.rem(z, 2) * 8 + x * 2 + c
    to_x = lax.div(z, 2)
    own = pltpu.make_async_copy(raw.at[c], rbuf.at[slot], r_recv)
    for k in range(1, 16):
        cc = lax.rem(c + k, 2)
        remote(raw.at[cc], rbuf.at[slot], r_send, r_recv, dev(y, lax.rem(z + k // 2, 8), to_x, cc)).start()
    first = remote(raw.at[c], rbuf.at[slot], r_send, r_recv, dev(y, z, to_x, c))

    @pl.when(mine)
    def _():
        own.start()

    @pl.when(jnp.logical_not(mine))
    def _():
        first.start()

    count = 40 * 1024

    def mean_to(b):
        stat[b, 0:8, :] = per_channel(per_group(sums[0], ind_ref[...], count), ind_ref[...])

    def scale_to(b):
        var = per_group(sums[1], ind_ref[...], count)
        stat[b, 8:16, :] = per_channel(lax.rsqrt(var + EPS), ind_ref[...])

    mean_to(0)

    @pl.loop(0, STEPS)
    def _(i):
        off = feat[rows_of(i), :].astype(F32) - stat[0, 0:1, :]
        sums[1] += eights(off * off)

    scale_to(0)
    emb[0] = embed((999 - 250 * s_step[0]).astype(F32), 640)
    emb[1] = embed(t_step[0].astype(F32), 640)

    rings = [Ring(b, y, z, x, c) for b in range(2)]

    def at(b, g):
        return wb.at[(b * 2 + c) * 16 + g]

    def send(b, g, device):
        remote(at(b, g), at(b, g), s_send.at[b], s_recv.at[b, g], device).start()

    def hand(b, g):
        remote(at(b, g), at(b, g), s_send.at[b], s_sib.at[b], dev(y, z, x, 1 - c)).start()

    def wait(b, g):
        remote(at(b, g), at(b, g), s_send.at[b], s_recv.at[b, g], dev(y, z, x, 1 - c)).wait_recv()

    pltpu.make_async_copy(rbuf, rbuf, r_recv).wait()
    row = lax.broadcasted_iota(jnp.int32, (16, 128), 0)
    for b in range(2):
        ring = rings[b]
        g = ring.block(0, 0)
        k = (b * 2 + c) * 16 + g
        outs = []
        for h in range(2):
            t = 2 * b + h
            tile = rbuf[:, 16 * t : 16 * t + 16, :].reshape(256, 128)
            out = jnp.dot(sel_ref[...], tile, preferred_element_type=F32)
            outs.append(out[240:256])
            for i in range(3):
                j = 3 * h + i
                if j < 5:
                    wb[k, 80 * j : 80 * j + 80, :] = out[80 * i : 80 * i + 80].astype(BF16)
        wb[k, 400:416, :] = jnp.where(row == 0, outs[0], outs[1]).astype(BF16)
        send(b, g, ring.first(1))
        send(b, g, ring.first(3))
        send(b, g, ring.second(1))
        send(b, g, ring.second(3))
        hand(b, g)

    def gather_first(b):
        ring = rings[b]
        for d in (3, 1, 2):
            g = ring.block(d, 0)
            wait(b, g)
            if d == (3 if b == 0 else 1):
                send(b, g, ring.first(1 if b == 0 else 3))
            send(b, g, ring.second(1))
            send(b, g, ring.second(3))
            hand(b, g)

    def gather_second(b, n):
        ring = rings[b]
        d = (0, 3, 1, 2)[n]
        for e in (3, 1):
            g = ring.block(d, e)
            wait(b, g)
            if e == (3 if n % 2 == 0 else 1):
                send(b, g, ring.second(1 if e == 3 else 3))
            hand(b, g)

    def gather_last(b):
        for d in (0, 3, 1, 2):
            g = rings[b].block(d, 2)
            wait(b, g)
            hand(b, g)

    def gathered(b):
        pltpu.make_async_copy(wb.at[pl.ds(0, 16)], wb.at[pl.ds(0, 16)], s_sib.at[b]).wait()
        for n in (2 * b, 2 * b + 1):
            for j in range(5):
                w[n, :, 128 * j : 128 * j + 128] = wb[16 * n : 16 * n + 16, 80 * j : 80 * j + 80, :].reshape(1280, 128)
        lane = lax.broadcasted_iota(jnp.int32, (16, 128), 1)
        parts = [jnp.zeros((16, 128), F32) for _ in range(10)]
        for g in range(16):
            tile, s = divmod(80 * g, 128)
            v = wb[2 * b * 16 + g, 400:416, :].astype(F32)
            if s:
                v = pltpu.roll(v, s, 1)
            parts[tile] += jnp.where(lane >= s, v, 0.0)
            if s + 80 > 128:
                parts[tile + 1] += jnp.where(lane < s, v, 0.0)
        for n in range(10):
            vec[b, :, 128 * n : 128 * n + 128] = parts[n]

    gather_first(0)
    gather_first(1)
    for n in range(4):
        gather_second(0, n)
    gather_last(0)
    gathered(0)

    keep = plan_of(t_step[0])
    root, other_root = jnp.sqrt(keep), jnp.sqrt(1.0 - keep)
    nt = (((1,), (1,)), ((), ()))
    sums[...] = jnp.zeros_like(sums)
    loads[1].wait()

    @pl.loop(0, STEPS)
    def _(i):
        s = rows_of(i)
        field = feat[s, :].astype(F32)
        normed = (field - stat[0, 0:1, :]) * stat[0, 8:9, :]
        hid[s, :] = (normed * vec[0, 0:1, :] + vec[0, 1:2, :]).astype(BF16)
        u = jnp.dot(hid[s, :], w[0], preferred_element_type=F32) + emb[0, 0:1, :]
        pre[s, :] = u
        act[s, :] = (u * jax.nn.sigmoid(u)).astype(BF16)
        out = field + lax.dot_general(act[s, :], w[1], nt, preferred_element_type=F32)
        sample[s, :] = out
        noisy = (root * out + other_root * noise[s, :].astype(F32)).astype(BF16)
        noise[s, :] = noisy
        sums[0] += eights(noisy.astype(F32))
        for n in range(4):

            @pl.when(i == n)
            def _(n=n):
                gather_second(1, n)

    gather_last(1)
    mean_to(1)

    @pl.loop(0, STEPS)
    def _(i):
        off = noise[rows_of(i), :].astype(F32) - stat[1, 0:1, :]
        sums[1] += eights(off * off)

    scale_to(1)
    gathered(1)
    loads[2].wait()

    norm = 1.0 / 512.0

    @pl.loop(0, STEPS)
    def _(i):
        s = rows_of(i)
        field = noise[s, :].astype(F32)
        normed = (field - stat[1, 0:1, :]) * stat[1, 8:9, :]
        h = (normed * vec[1, 0:1, :] + vec[1, 1:2, :]).astype(BF16)
        u = jnp.dot(h, w[2], preferred_element_type=F32) + emb[1, 0:1, :]
        a = (u * jax.nn.sigmoid(u)).astype(BF16)
        target = field + lax.dot_general(a, w[3], nt, preferred_element_type=F32)
        critic[s, :] = ((2.0 * keep * (sample[s, :] - target) + critic[s, :].astype(F32)) * norm).astype(BF16)

    def to_sibling(b, g):
        return remote(grad.at[b, g, 1 - c], sib.at[b, g], h_send.at[b], h_recv.at[b, g], dev(y, z, x, 1 - c))

    def term(b, left, right):
        for tile in range(2):
            out = lax.dot_general(
                left[:, 640 * tile : 640 * tile + 640], right[...], (((0,), (0,)), ((), ())), preferred_element_type=F32
            )
            for n in range(8):
                for h in range(2):
                    for j in range(5):
                        grad[b, 8 * tile + n, h, 40 * j : 40 * j + 40, :] = out[
                            80 * n + 40 * h : 80 * n + 40 * h + 40, 128 * j : 128 * j + 128
                        ]
            for n in range(8):
                to_sibling(b, 8 * tile + n).start()

    for g in range(16):
        for h in range(2):
            grad[0, g, h, 200:208, :] = jnp.zeros((8, 128), F32)
    term(0, critic, act)

    def meet(b, g):
        to_sibling(b, g).wait_recv()
        sib[b, g] += grad[b, g, c]

    def push(b, g, dst, recv, d):
        remote(sib.at[b, g], dst, q_send.at[b], recv, rings[b].second(d)).start()

    def reduce_far(b):
        for k in range(4):
            g = rings[b].block((2, 1, 3, 0)[k], 2)
            meet(b, g)
            push(b, g, t1.at[b, k], t_recv.at[b, k], 1 if k % 2 == 0 else 3)

    def reduce_near(b, k):
        d = (2, 1, 3, 0)[k]
        for e in (3, 1) if k % 2 == 0 else (1, 3):
            g = rings[b].block(d, e)
            meet(b, g)
            if e == (1 if k % 2 == 0 else 3):
                remote(t1.at[b, k], t1.at[b, k], q_send.at[b], t_recv.at[b, k], rings[b].second(1)).wait_recv()
                sib[b, g] += t1[b, k]
            if e == 1:
                push(b, g, fm.at[b, k], m_recv.at[b, k], 1)
            else:
                push(b, g, fp.at[b, k], p_recv.at[b, k], 3)

    def arrive(b, dst, recv):
        remote(dst, dst, p_send.at[b], recv, rings[b].first(1)).wait_recv()

    def reduce_first(b, k):
        ring = rings[b]

        def push1(dst, recv, d):
            remote(acc.at[b, k], dst, p_send.at[b], recv, ring.first(d)).start()

        d = (2, 1, 3, 0)[k] if b == 0 else (2, 3, 1, 0)[k]
        kk = (2, 1, 3, 0).index(d)
        g = ring.block(d, 0)
        meet(b, g)
        arrive(b, fm.at[b, kk], m_recv.at[b, kk])
        arrive(b, fp.at[b, kk], p_recv.at[b, kk])
        acc[b, k] = sib[b, g] + fm[b, kk] + fp[b, kk]
        if k == 0:
            push1(u1.at[b], ut_recv.at[b], 1 if b == 0 else 3)
        if k == 1:
            arrive(b, u1.at[b], ut_recv.at[b])
            acc[b, k] += u1[b]
        if k in (1, 2):
            if d == 1:
                push1(um.at[b], um_recv.at[b], 1)
            else:
                push1(up.at[b], up_recv.at[b], 3)

    def pieces(b):
        arrive(b, um.at[b], um_recv.at[b])
        arrive(b, up.at[b], up_recv.at[b])
        total = acc[b, 3] + um[b] + up[b]
        for s in range(8):
            for j in range(5):
                stage[b, s, 0:5, 128 * j : 128 * j + 128] = total[40 * j + 5 * s : 40 * j + 5 * s + 5]
            v = total[200:208]
            if s:
                v = pltpu.roll(v, 128 - 5 * s, 1)
            stage[b, s, 5:7, 0:128] = v[0:2]
        for k in range(1, 8):
            s = lax.rem(x * 2 + c + k, 8)
            remote(
                stage.at[b, s], fin.at[b, z], f_send.at[b], f_recv.at[b],
                dev(y, 2 * x + c, lax.div(s, 2), lax.rem(s, 2)),
            ).start()
        s = x * 2 + c
        stay = pltpu.make_async_copy(stage.at[b, s], fin.at[b, z], f_recv.at[b])
        go = remote(stage.at[b, s], fin.at[b, z], f_send.at[b], f_recv.at[b], dev(y, 2 * x + c, x, c))

        @pl.when(selfish)
        def _():
            stay.start()

        @pl.when(jnp.logical_not(selfish))
        def _():
            go.start()

    sums[...] = jnp.zeros_like(sums)

    @pl.loop(0, STEPS)
    def _(i):
        s = rows_of(i)
        d_act = jnp.dot(critic[s, :], w[1], preferred_element_type=F32)
        u = pre[s, :]
        sig = jax.nn.sigmoid(u)
        dp = (d_act * sig * (1.0 + u * (1.0 - sig))).astype(BF16)
        dpre[s, :] = dp
        d_hid = lax.dot_general(dp, w[0], nt, preferred_element_type=F32)
        normed = (feat[s, :].astype(F32) - stat[0, 0:1, :]) * stat[0, 8:9, :]
        sums[0] += eights(d_hid * normed)
        sums[1] += eights(d_hid)

        @pl.when(i == 0)
        def _():
            reduce_far(0)

        @pl.when(i == 2)
        def _():
            reduce_near(0, 0)
            reduce_near(0, 1)

        @pl.when(i == 3)
        def _():
            reduce_near(0, 2)
            reduce_near(0, 3)

    top = lax.broadcasted_iota(jnp.int32, (8, 128), 0) == 0
    lane8 = lax.broadcasted_iota(jnp.int32, (8, 128), 1)
    lines = []
    for n in range(10):
        gains = jnp.sum(sums[0, :, 128 * n : 128 * n + 128], axis=0, keepdims=True)
        shifts = jnp.sum(sums[1, :, 128 * n : 128 * n + 128], axis=0, keepdims=True)
        lines.append(jnp.where(top, gains, shifts))
    for n in range(32):
        tile, s = divmod(40 * n, 128)
        v = pltpu.roll(lines[tile], 128 - s, 1) if s else lines[tile]
        if s + 40 > 128:
            v = jnp.where(lane8 < 128 - s, v, pltpu.roll(lines[tile + 1], 128 - s, 1))
        grad[1, n // 2, n % 2, 200:208, :] = v
    term(1, hid, dpre)

    for k in range(4):
        reduce_first(0, k)
    reduce_far(1)
    pieces(0)
    for k in range(4):
        reduce_near(1, k)
    for k in range(4):
        reduce_first(1, k)
    pieces(1)

    for b in range(2):
        pltpu.make_async_copy(fin.at[b], fin.at[b], f_recv.at[b]).wait()
        o_ref[b] = jnp.sum(fin[b], axis=0)

    @pl.when(mine)
    def _():
        pltpu.make_async_copy(rbuf.at[pl.ds(0, 15)], rbuf.at[pl.ds(0, 15)], r_send).wait()

    @pl.when(jnp.logical_not(mine))
    def _():
        pltpu.make_async_copy(rbuf, rbuf, r_send).wait()

    for b in range(2):
        pltpu.make_async_copy(wb.at[pl.ds(0, 31)], wb.at[pl.ds(0, 31)], s_send.at[b]).wait()
        pltpu.make_async_copy(sib.at[b], sib.at[b], h_send.at[b]).wait()
        pltpu.make_async_copy(sib.at[b, pl.ds(0, 12)], sib.at[b, pl.ds(0, 12)], q_send.at[b]).wait()
        pltpu.make_async_copy(acc.at[b, pl.ds(0, 3)], acc.at[b, pl.ds(0, 3)], p_send.at[b]).wait()

        @pl.when(selfish)
        def _():
            pltpu.make_async_copy(fin.at[b, pl.ds(0, 7)], fin.at[b, pl.ds(0, 7)], f_send.at[b]).wait()

        @pl.when(jnp.logical_not(selfish))
        def _():
            pltpu.make_async_copy(fin.at[b], fin.at[b], f_send.at[b]).wait()


def selection():
    sel = np.zeros((256, 256), np.float32)
    for m in range(240):
        i, q = divmod(m, 80)
        sel[m, 16 * (q // 5) + 5 * i + q % 5] = 1.0
    for d in range(16):
        sel[240:242, 16 * d + 15] = 1.0
    return jnp.asarray(sel, BF16)


def membership():
    ind = np.zeros((1280, 128), np.float32)
    ind[np.arange(1280), np.arange(1280) // 40] = 1.0
    return jnp.asarray(ind, BF16)


def local(
    features,
    renoise,
    critic_grad,
    student_step,
    teacher_step,
    student_in,
    student_gain,
    student_shift,
    student_out,
    teacher_in,
    teacher_gain,
    teacher_shift,
    teacher_out,
):
    vecs = jnp.stack([student_gain, student_shift, teacher_gain, teacher_shift]).astype(F32)
    vecs = jnp.pad(vecs, ((0, 4), (0, 123)))
    vmem = pl.BlockSpec(memory_space=pltpu.VMEM)
    smem = pl.BlockSpec(memory_space=pltpu.SMEM)
    hbm = pl.BlockSpec(memory_space=pl.ANY)
    half = (208, 128)
    dma = pltpu.SemaphoreType.DMA
    out = pl.pallas_call(
        kernel,
        out_shape=jax.ShapeDtypeStruct((2, 8, 640), F32),
        in_specs=[hbm] * 3 + [smem] * 2 + [vmem] * 7,
        out_specs=vmem,
        scratch_shapes=[
            pltpu.VMEM((1024, 1280), BF16),
            pltpu.VMEM((1024, 1280), BF16),
            pltpu.VMEM((1024, 1280), BF16),
            pltpu.VMEM((2, 64, 128), F32),
            pltpu.VMEM((2, 64, 128), BF16),
            pltpu.VMEM((16, 64, 128), BF16),
            pltpu.VMEM((64, 416, 128), BF16),
            pltpu.VMEM((4, 1280, 640), BF16),
            pltpu.VMEM((2, 16, 1280), F32),
            pltpu.VMEM((1024, 1280), BF16),
            pltpu.VMEM((1024, 640), F32),
            pltpu.VMEM((1024, 640), BF16),
            pltpu.VMEM((1024, 1280), F32),
            pltpu.VMEM((1024, 640), BF16),
            pltpu.VMEM((2, 8, 1280), F32),
            pltpu.VMEM((2, 16, 1280), F32),
            pltpu.VMEM((2, 8, 640), F32),
            pltpu.VMEM((2, 16, 2, *half), F32),
            pltpu.VMEM((2, 16, *half), F32),
            pltpu.VMEM((2, 4, *half), F32),
            pltpu.VMEM((2, 4, *half), F32),
            pltpu.VMEM((2, 4, *half), F32),
            pltpu.VMEM((2, 4, *half), F32),
            pltpu.VMEM((2, *half), F32),
            pltpu.VMEM((2, *half), F32),
            pltpu.VMEM((2, *half), F32),
            pltpu.VMEM((2, 8, 8, 640), F32),
            pltpu.VMEM((2, 8, 8, 640), F32),
            dma((3,)),
            dma,
            dma,
            dma((2,)),
            dma((2, 16)),
            dma((2,)),
            dma((2,)),
            dma((2, 16)),
            dma((2,)),
            dma((2, 4)),
            dma((2, 4)),
            dma((2, 4)),
            dma((2,)),
            dma((2,)),
            dma((2,)),
            dma((2,)),
            dma((2,)),
            dma((2,)),
        ],
        compiler_params=pltpu.CompilerParams(collective_id=0, has_side_effects=True, vmem_limit_bytes=62 * 2**20),
    )(
        features, renoise, critic_grad, student_step, teacher_step, student_in, student_out.T, teacher_in, teacher_out.T,
        vecs, selection(), membership(),
    )
    return out[1, :5], out[0, :5].T, out[1, 5, :5], out[1, 6, :5]


def solution(mesh):
    return jax.shard_map(
        local,
        mesh=mesh,
        in_specs=(
            P("dp", None, None),
            P("dp", None, None),
            P("dp", None, None),
            P("dp"),
            P("dp"),
            P("dp", None),
            P("dp"),
            P("dp"),
            P(None, "dp"),
            P("dp", None),
            P("dp"),
            P("dp"),
            P(None, "dp"),
        ),
        out_specs=(P("dp", None), P(None, "dp"), P("dp"), P("dp")),
        check_vma=False,
    )
```

```python
import functools
import math

import jax
import jax.numpy as jnp
import numpy as np
from jax import lax
from jax.experimental import pallas as pl
from jax.experimental.pallas import tpu as pltpu
from jax.sharding import PartitionSpec as P

GROUPS = 32
STEPS_T = 1000
EPS = 1e-05
MESH = pl.DeviceIdType.MESH
F32 = jnp.float32
BF16 = jnp.bfloat16


def dev(y, z, x, c):
    return ((y * 8 + z) * 4 + x) * 2 + c


def where_am_i():
    me = lax.axis_index("dp")
    c = lax.rem(me, 2)
    x = lax.rem(lax.div(me, 2), 4)
    z = lax.rem(lax.div(me, 8), 8)
    y = lax.div(me, 64)
    return y, z, x, c


class Ring:
    def __init__(self, b, y, z, x, c):
        r = lax.rem(c + b, 2)
        self.r = r
        self.p = (1 - r) * y + r * x
        self.q = (1 - r) * x + r * y
        self.at = (y, z, x, c)

    def block(self, dp, dq):
        pp = lax.rem(self.p + dp, 4)
        qq = lax.rem(self.q + dq, 4)
        return pp * (4 - 3 * self.r) + qq * (1 + 3 * self.r)

    def first(self, d):
        y, z, x, c = self.at
        r = self.r
        return dev(lax.rem(y + (1 - r) * d, 4), z, lax.rem(x + r * d, 4), c)

    def second(self, d):
        y, z, x, c = self.at
        r = self.r
        return dev(lax.rem(y + r * d, 4), z, lax.rem(x + (1 - r) * d, 4), c)


def signal(device):
    pl.semaphore_signal(pltpu.get_barrier_semaphore(), inc=1, device_id=(device,), device_id_type=MESH)


def remote(src, dst, ssem, rsem, device):
    return pltpu.make_async_remote_copy(
        src_ref=src, dst_ref=dst, send_sem=ssem, recv_sem=rsem, device_id=(device,), device_id_type=MESH
    )


def greet_planes(y, z, x, c):
    for d in (1, 2, 3):
        signal(dev(y, z, lax.rem(x + d, 4), c))
        signal(dev(lax.rem(y + d, 4), z, x, c))
    signal(dev(y, z, x, 1 - c))


ROWS = 256
STEPS = 4


def plan_of(step):
    index = lax.broadcasted_iota(jnp.int32, (8, 128), 0) * 128 + lax.broadcasted_iota(jnp.int32, (8, 128), 1)
    lo = math.sqrt(0.00085)
    hi = math.sqrt(0.012)
    betas = (lo + (hi - lo) * index.astype(F32) / (STEPS_T - 1)) ** 2
    logs = jnp.where(index <= step, jnp.log(1.0 - betas), 0.0)
    return jnp.exp(jnp.sum(jnp.sum(logs, axis=1, keepdims=True), axis=0, keepdims=True))


def embed(tval, width):
    half = width // 2
    lane = lax.broadcasted_iota(jnp.int32, (8, width), 1)
    index = jnp.where(lane < half, lane, lane - half).astype(F32)
    angles = tval * jnp.exp(-math.log(10000.0) * index / half)
    return jnp.where(lane < half, jnp.cos(angles), jnp.sin(angles))


def by_parts(value, indicator, dims):
    total = None
    for _ in range(3):
        part = value.astype(BF16)
        value = value - part.astype(F32)
        term = lax.dot_general(part, indicator, (dims, ((), ())), preferred_element_type=F32)
        total = term if total is None else total + term
    return total


def per_group(sums, indicator, count):
    groups = by_parts(sums, indicator, ((1,), (0,)))
    return jnp.broadcast_to(jnp.sum(groups, axis=0, keepdims=True), groups.shape) / count


def per_channel(groups, indicator):
    return by_parts(groups, indicator, ((1,), (1,)))


def eights(value):
    return jnp.sum(value.reshape(value.shape[0] // 8, 8, value.shape[1]), axis=0)


def kernel(
    feat_hbm, noise_hbm, critic_hbm, s_step, t_step, si_ref, so_ref, ti_ref, to_ref, sg_ref, ss_ref, tg_ref, ts_ref, sel_ref, ind_ref,
    in_ref, out_ref, gain_ref, shift_ref,
    feat, noise, critic, vecs, rawf, raw, rbuf, wb, w, vec, hid, pre, act, sample, dpre, sums, stat, emb,
    grad, sib, t1, fm, fp, acc, u1, um, up, stage, mid, fin,
    l_sem, r_send, r_recv, s_send, s_recv, s_sib,
    h_send, h_recv, q_send, t_recv, m_recv, p_recv, p_send, ut_recv, um_recv, up_recv, e_send, e_recv, f_send, f_recv,
):
    y, z, x, c = where_am_i()
    mine = lax.div(z, 2) == x
    loads = [
        pltpu.make_async_copy(src.at[0], dst, l_sem.at[n])
        for n, (src, dst) in enumerate(((feat_hbm, feat), (noise_hbm, noise), (critic_hbm, critic)))
    ]
    loads[0].start()

    greet_planes(y, z, x, c)
    for k in range(1, 16):
        signal(dev(y, 2 * x + lax.rem(z + k // 8, 2), lax.rem(x + k // 2, 4), lax.rem(c + k, 2)))

    @pl.when(jnp.logical_not(mine))
    def _():
        signal(dev(y, 2 * x + lax.rem(z, 2), x, c))

    for d in (1, 2, 3):
        signal(dev(y, z, lax.rem(x + d, 4), 1 - c))
    for k in range(1, 8):
        signal(dev(y, lax.rem(z + k, 8), x, c))

    rawf[...] = jnp.zeros_like(rawf)
    place = 5 * lax.rem(lax.axis_index("dp"), 16)
    vecs[...] = jnp.zeros_like(vecs)
    for n, ref in enumerate((sg_ref, ss_ref, tg_ref, ts_ref)):
        vecs[n : n + 1, 0:5] = ref[...].astype(F32)
    spread = pltpu.roll(vecs[...], place, 1)
    for core, pair in enumerate(((si_ref, ti_ref), (so_ref, to_ref))):
        for b, ref in enumerate(pair):
            shard = ref[...].astype(F32)
            for j in range(5):
                r = 16 * (2 * b + j // 3) + 5 * (j % 3)
                rawf[core, r : r + 5, :] = shard[:, 128 * j : 128 * j + 128]
            for h in range(2):
                r = 16 * (2 * b + h) + 15
                rawf[core, r : r + 1, :] = spread[2 * b + h : 2 * b + h + 1]
    raw[...] = rawf[...].astype(BF16)
    loads[0].wait()
    loads[1].start()
    loads[2].start()

    def rows_of(i):
        return pl.ds(pl.multiple_of(i * ROWS, ROWS), ROWS)

    sums[...] = jnp.zeros_like(sums)

    @pl.loop(0, STEPS)
    def _(i):
        sums[0] += eights(feat[rows_of(i), :].astype(F32))

    pl.semaphore_wait(pltpu.get_barrier_semaphore(), jnp.where(mine, 32, 33))

    slot = lax.rem(z, 2) * 8 + x * 2 + c
    to_x = lax.div(z, 2)
    for b in range(2):

        def shard(cc):
            return raw.at[cc, pl.ds(32 * b, 32)]

        for k in range(1, 16):
            cc = lax.rem(c + k, 2)
            remote(
                shard(cc), rbuf.at[b, slot], r_send.at[b], r_recv.at[b], dev(y, lax.rem(z + k // 2, 8), to_x, cc)
            ).start()
        own = pltpu.make_async_copy(shard(c), rbuf.at[b, slot], r_recv.at[b])
        first = remote(shard(c), rbuf.at[b, slot], r_send.at[b], r_recv.at[b], dev(y, z, to_x, c))

        @pl.when(mine)
        def _():
            own.start()

        @pl.when(jnp.logical_not(mine))
        def _():
            first.start()

    count = 40 * 1024

    def mean_to(b):
        stat[b, 0:8, :] = per_channel(per_group(sums[0], ind_ref[...], count), ind_ref[...])

    def scale_to(b):
        var = per_group(sums[1], ind_ref[...], count)
        stat[b, 8:16, :] = per_channel(lax.rsqrt(var + EPS), ind_ref[...])

    mean_to(0)

    @pl.loop(0, STEPS)
    def _(i):
        off = feat[rows_of(i), :].astype(F32) - stat[0, 0:1, :]
        sums[1] += eights(off * off)

    scale_to(0)
    emb[0] = embed((999 - 250 * s_step[0]).astype(F32), 640)
    emb[1] = embed(t_step[0].astype(F32), 640)

    rings = [Ring(b, y, z, x, c) for b in range(2)]

    def at(b, g):
        return wb.at[(b * 2 + c) * 16 + g]

    def send(b, g, device):
        remote(at(b, g), at(b, g), s_send.at[b], s_recv.at[b, g], device).start()

    def hand(b, g):
        remote(at(b, g), at(b, g), s_send.at[b], s_sib.at[b], dev(y, z, x, 1 - c)).start()

    def wait(b, g):
        remote(at(b, g), at(b, g), s_send.at[b], s_recv.at[b, g], dev(y, z, x, 1 - c)).wait_recv()

    row = lax.broadcasted_iota(jnp.int32, (16, 128), 0)
    for b in range(2):
        ring = rings[b]
        g = ring.block(0, 0)
        k = (b * 2 + c) * 16 + g
        pltpu.make_async_copy(rbuf.at[b], rbuf.at[b], r_recv.at[b]).wait()
        outs = []
        for h in range(2):
            tile = rbuf[b, :, 16 * h : 16 * h + 16, :].reshape(256, 128)
            out = jnp.dot(sel_ref[...], tile, preferred_element_type=F32)
            outs.append(out[240:256])
            for i in range(3):
                j = 3 * h + i
                if j < 5:
                    wb[k, 80 * j : 80 * j + 80, :] = out[80 * i : 80 * i + 80].astype(BF16)
        wb[k, 400:416, :] = jnp.where(row == 0, outs[0], outs[1]).astype(BF16)
        send(b, g, ring.first(1))
        send(b, g, ring.first(3))
        send(b, g, ring.first(2))
        send(b, g, ring.second(1))
        send(b, g, ring.second(3))
        hand(b, g)

    def gather_first(b):
        ring = rings[b]
        for d in (3, 1, 2):
            g = ring.block(d, 0)
            wait(b, g)
            send(b, g, ring.second(1))
            send(b, g, ring.second(3))
            hand(b, g)

    def gather_second(b, n, e):
        ring = rings[b]
        g = ring.block((0, 3, 1, 2)[n], e)
        wait(b, g)
        if e == (3 if n % 2 == 0 else 1):
            send(b, g, ring.second(1 if e == 3 else 3))
        hand(b, g)

    def gather_last(b):
        for d in (0, 3, 1, 2):
            g = rings[b].block(d, 2)
            wait(b, g)
            hand(b, g)

    def gathered(b):
        pltpu.make_async_copy(wb.at[pl.ds(0, 16)], wb.at[pl.ds(0, 16)], s_sib.at[b]).wait()
        for n in (2 * b, 2 * b + 1):
            for j in range(5):
                w[n, :, 128 * j : 128 * j + 128] = wb[16 * n : 16 * n + 16, 80 * j : 80 * j + 80, :].reshape(1280, 128)
        lane = lax.broadcasted_iota(jnp.int32, (16, 128), 1)
        parts = [jnp.zeros((16, 128), F32) for _ in range(10)]
        for g in range(16):
            tile, s = divmod(80 * g, 128)
            v = wb[2 * b * 16 + g, 400:416, :].astype(F32)
            if s:
                v = pltpu.roll(v, s, 1)
            parts[tile] += jnp.where(lane >= s, v, 0.0)
            if s + 80 > 128:
                parts[tile + 1] += jnp.where(lane < s, v, 0.0)
        for n in range(10):
            vec[b, :, 128 * n : 128 * n + 128] = parts[n]

    gather_first(0)
    gather_first(1)
    for n in range(4):
        gather_second(0, n, 3)
        gather_second(0, n, 1)
    gather_last(0)
    gathered(0)

    keep = plan_of(t_step[0])
    root, other_root = jnp.sqrt(keep), jnp.sqrt(1.0 - keep)
    nt = (((1,), (1,)), ((), ()))
    sums[...] = jnp.zeros_like(sums)
    loads[1].wait()

    @pl.loop(0, STEPS)
    def _(i):
        s = rows_of(i)
        field = feat[s, :].astype(F32)
        normed = (field - stat[0, 0:1, :]) * stat[0, 8:9, :]
        hid[s, :] = (normed * vec[0, 0:1, :] + vec[0, 1:2, :]).astype(BF16)
        u = jnp.dot(hid[s, :], w[0], preferred_element_type=F32) + emb[0, 0:1, :]
        pre[s, :] = u
        act[s, :] = (u * jax.nn.sigmoid(u)).astype(BF16)
        for n in range(4):

            @pl.when(i == n)
            def _(n=n):
                gather_second(1, n, 3)

        out = field + lax.dot_general(act[s, :], w[1], nt, preferred_element_type=F32)
        sample[s, :] = out
        noisy = (root * out + other_root * noise[s, :].astype(F32)).astype(BF16)
        noise[s, :] = noisy
        sums[0] += eights(noisy.astype(F32))
        for n in range(4):

            @pl.when(i == n)
            def _(n=n):
                gather_second(1, n, 1)

    gather_last(1)
    mean_to(1)

    @pl.loop(0, STEPS)
    def _(i):
        off = noise[rows_of(i), :].astype(F32) - stat[1, 0:1, :]
        sums[1] += eights(off * off)

    scale_to(1)
    gathered(1)
    loads[2].wait()

    norm = 1.0 / 512.0

    @pl.loop(0, STEPS)
    def _(i):
        s = rows_of(i)
        field = noise[s, :].astype(F32)
        normed = (field - stat[1, 0:1, :]) * stat[1, 8:9, :]
        h = (normed * vec[1, 0:1, :] + vec[1, 1:2, :]).astype(BF16)
        u = jnp.dot(h, w[2], preferred_element_type=F32) + emb[1, 0:1, :]
        a = (u * jax.nn.sigmoid(u)).astype(BF16)
        target = field + lax.dot_general(a, w[3], nt, preferred_element_type=F32)
        critic[s, :] = ((2.0 * keep * (sample[s, :] - target) + critic[s, :].astype(F32)) * norm).astype(BF16)

    def to_sibling(b, g):
        return remote(grad.at[b, g, 1 - c], sib.at[b, g], h_send.at[b], h_recv.at[b, g], dev(y, z, x, 1 - c))

    def term(b, left, right):
        for tile in range(2):
            out = lax.dot_general(
                left[:, 640 * tile : 640 * tile + 640], right[...], (((0,), (0,)), ((), ())), preferred_element_type=F32
            )
            for n in range(8):
                for h in range(2):
                    for j in range(5):
                        grad[b, 8 * tile + n, h, 40 * j : 40 * j + 40, :] = out[
                            80 * n + 40 * h : 80 * n + 40 * h + 40, 128 * j : 128 * j + 128
                        ]
            for n in range(8):
                to_sibling(b, 8 * tile + n).start()

    for g in range(16):
        for h in range(2):
            grad[0, g, h, 200:208, :] = jnp.zeros((8, 128), F32)
    term(0, critic, act)

    def meet(b, g, *more):
        to_sibling(b, g).wait_recv()
        total = sib[b, g] + grad[b, g, c]
        for ref in more:
            total += ref[...]
        return total

    def push(b, g, dst, recv, d):
        remote(sib.at[b, g], dst, q_send.at[b], recv, rings[b].second(d)).start()

    def reduce_far(b):
        for k in range(4):
            g = rings[b].block((2, 1, 3, 0)[k], 2)
            sib[b, g] = meet(b, g)
            push(b, g, t1.at[b, k], t_recv.at[b, k], 1 if k % 2 == 0 else 3)

    def reduce_direct(b):
        for k in range(4):
            e = 3 if k % 2 == 0 else 1
            g = rings[b].block((2, 1, 3, 0)[k], e)
            sib[b, g] = meet(b, g)
            if e == 1:
                push(b, g, fm.at[b, k], m_recv.at[b, k], 1)
            else:
                push(b, g, fp.at[b, k], p_recv.at[b, k], 3)

    def reduce_through(b):
        for k in range(4):
            e = 1 if k % 2 == 0 else 3
            g = rings[b].block((2, 1, 3, 0)[k], e)
            remote(t1.at[b, k], t1.at[b, k], q_send.at[b], t_recv.at[b, k], rings[b].second(1)).wait_recv()
            sib[b, g] = meet(b, g, t1.at[b, k])
            if e == 1:
                push(b, g, fm.at[b, k], m_recv.at[b, k], 1)
            else:
                push(b, g, fp.at[b, k], p_recv.at[b, k], 3)

    def arrive(b, dst, recv):
        remote(dst, dst, p_send.at[b], recv, rings[b].first(1)).wait_recv()

    def reduce_first(b, k):
        g = rings[b].block((2, 1, 3, 0)[k], 0)
        arrive(b, fm.at[b, k], m_recv.at[b, k])
        arrive(b, fp.at[b, k], p_recv.at[b, k])
        acc[b, k] = meet(b, g, fm.at[b, k], fp.at[b, k])
        if k < 3:
            dst, recv, d = ((u1, ut_recv, 2), (um, um_recv, 1), (up, up_recv, 3))[k]
            remote(acc.at[b, k], dst.at[b], p_send.at[b], recv.at[b], rings[b].first(d)).start()

    def pieces(b):
        arrive(b, um.at[b], um_recv.at[b])
        arrive(b, up.at[b], up_recv.at[b])
        arrive(b, u1.at[b], ut_recv.at[b])
        total = acc[b, 3] + um[b] + up[b] + u1[b]
        here = x * 2 + c
        for s in range(8):
            for j in range(5):
                stage[b, s, 0:5, 128 * j : 128 * j + 128] = total[40 * j + 5 * s : 40 * j + 5 * s + 5]
            v = total[200:208]
            if s:
                v = pltpu.roll(v, 128 - 5 * s, 1)
            stage[b, s, 5:7, 0:128] = v[0:2]

            @pl.when(here != s)
            def _(s=s):
                remote(
                    stage.at[b, s], mid.at[b, here], e_send.at[b], e_recv.at[b], dev(y, z, s // 2, s % 2)
                ).start()

            @pl.when(here == s)
            def _(s=s):
                pltpu.make_async_copy(stage.at[b, s], mid.at[b, here], e_recv.at[b]).start()

    def spread_pieces(b):
        pltpu.make_async_copy(mid.at[b], mid.at[b], e_recv.at[b]).wait()
        for k in (4, 3, 5, 2, 6, 1, 7):
            to = lax.rem(z + k, 8)
            remote(mid.at[b, to], fin.at[b, z], f_send.at[b], f_recv.at[b], dev(y, to, x, c)).start()
        pltpu.make_async_copy(mid.at[b, z], fin.at[b, z], f_recv.at[b]).start()

    sums[...] = jnp.zeros_like(sums)

    @pl.loop(0, STEPS)
    def _(i):
        s = rows_of(i)
        d_act = jnp.dot(critic[s, :], w[1], preferred_element_type=F32)
        u = pre[s, :]
        sig = jax.nn.sigmoid(u)
        dp = (d_act * sig * (1.0 + u * (1.0 - sig))).astype(BF16)
        dpre[s, :] = dp
        d_hid = lax.dot_general(dp, w[0], nt, preferred_element_type=F32)
        normed = (feat[s, :].astype(F32) - stat[0, 0:1, :]) * stat[0, 8:9, :]
        sums[0] += eights(d_hid * normed)
        sums[1] += eights(d_hid)

        @pl.when(i == 1)
        def _():
            reduce_far(0)

        @pl.when(i == 2)
        def _():
            reduce_direct(0)

        @pl.when(i == 3)
        def _():
            reduce_through(0)

    top = lax.broadcasted_iota(jnp.int32, (8, 128), 0) == 0
    lane8 = lax.broadcasted_iota(jnp.int32, (8, 128), 1)
    lines = []
    for n in range(10):
        gains = jnp.sum(sums[0, :, 128 * n : 128 * n + 128], axis=0, keepdims=True)
        shifts = jnp.sum(sums[1, :, 128 * n : 128 * n + 128], axis=0, keepdims=True)
        lines.append(jnp.where(top, gains, shifts))
    for n in range(32):
        tile, s = divmod(40 * n, 128)
        v = pltpu.roll(lines[tile], 128 - s, 1) if s else lines[tile]
        if s + 40 > 128:
            v = jnp.where(lane8 < 128 - s, v, pltpu.roll(lines[tile + 1], 128 - s, 1))
        grad[1, n // 2, n % 2, 200:208, :] = v
    term(1, hid, dpre)

    for k in range(4):
        reduce_first(0, k)
    reduce_far(1)
    reduce_direct(1)
    pieces(0)
    reduce_through(1)
    spread_pieces(0)
    for k in range(4):
        reduce_first(1, k)
    pieces(1)
    pltpu.make_async_copy(fin.at[0], fin.at[0], f_recv.at[0]).wait()
    out_ref[...] = jnp.sum(fin[0], axis=0)[0:5]
    spread_pieces(1)
    pltpu.make_async_copy(fin.at[1], fin.at[1], f_recv.at[1]).wait()
    total = jnp.sum(fin[1], axis=0)
    in_ref[...] = total[0:5]
    gain_ref[...] = total[5:6, 0:5]
    shift_ref[...] = total[6:7, 0:5]

    for b in range(2):

        @pl.when(mine)
        def _():
            pltpu.make_async_copy(rbuf.at[b, pl.ds(0, 15)], rbuf.at[b, pl.ds(0, 15)], r_send.at[b]).wait()

        @pl.when(jnp.logical_not(mine))
        def _():
            pltpu.make_async_copy(rbuf.at[b], rbuf.at[b], r_send.at[b]).wait()

        pltpu.make_async_copy(wb.at[pl.ds(0, 31)], wb.at[pl.ds(0, 31)], s_send.at[b]).wait()
        pltpu.make_async_copy(sib.at[b], sib.at[b], h_send.at[b]).wait()
        pltpu.make_async_copy(sib.at[b, pl.ds(0, 12)], sib.at[b, pl.ds(0, 12)], q_send.at[b]).wait()
        pltpu.make_async_copy(acc.at[b, pl.ds(0, 3)], acc.at[b, pl.ds(0, 3)], p_send.at[b]).wait()
        pltpu.make_async_copy(fin.at[b, pl.ds(0, 7)], fin.at[b, pl.ds(0, 7)], e_send.at[b]).wait()
        pltpu.make_async_copy(fin.at[b, pl.ds(0, 7)], fin.at[b, pl.ds(0, 7)], f_send.at[b]).wait()


def selection():
    sel = np.zeros((256, 256), np.float32)
    for m in range(240):
        i, q = divmod(m, 80)
        sel[m, 16 * (q // 5) + 5 * i + q % 5] = 1.0
    for d in range(16):
        sel[240:242, 16 * d + 15] = 1.0
    return jnp.asarray(sel, BF16)


def membership():
    ind = np.zeros((1280, 128), np.float32)
    ind[np.arange(1280), np.arange(1280) // 40] = 1.0
    return jnp.asarray(ind, BF16)


def local(
    features,
    renoise,
    critic_grad,
    student_step,
    teacher_step,
    student_in,
    student_gain,
    student_shift,
    student_out,
    teacher_in,
    teacher_gain,
    teacher_shift,
    teacher_out,
):
    vectors = [v[None, :] for v in (student_gain, student_shift, teacher_gain, teacher_shift)]
    vmem = pl.BlockSpec(memory_space=pltpu.VMEM)
    smem = pl.BlockSpec(memory_space=pltpu.SMEM)
    hbm = pl.BlockSpec(memory_space=pl.ANY)
    half = (208, 128)
    dma = pltpu.SemaphoreType.DMA
    grad_in, grad_out_t, grad_gain, grad_shift = pl.pallas_call(
        kernel,
        out_shape=[jax.ShapeDtypeStruct(shape, F32) for shape in ((5, 640), (5, 640), (1, 5), (1, 5))],
        in_specs=[hbm] * 3 + [smem] * 2 + [vmem] * 10,
        out_specs=[vmem] * 4,
        scratch_shapes=[
            pltpu.VMEM((1024, 1280), BF16),
            pltpu.VMEM((1024, 1280), BF16),
            pltpu.VMEM((1024, 1280), BF16),
            pltpu.VMEM((8, 128), F32),
            pltpu.VMEM((2, 64, 128), F32),
            pltpu.VMEM((2, 64, 128), BF16),
            pltpu.VMEM((2, 16, 32, 128), BF16),
            pltpu.VMEM((64, 416, 128), BF16),
            pltpu.VMEM((4, 1280, 640), BF16),
            pltpu.VMEM((2, 16, 1280), F32),
            pltpu.VMEM((1024, 1280), BF16),
            pltpu.VMEM((1024, 640), F32),
            pltpu.VMEM((1024, 640), BF16),
            pltpu.VMEM((1024, 1280), F32),
            pltpu.VMEM((1024, 640), BF16),
            pltpu.VMEM((2, 8, 1280), F32),
            pltpu.VMEM((2, 16, 1280), F32),
            pltpu.VMEM((2, 8, 640), F32),
            pltpu.VMEM((2, 16, 2, *half), F32),
            pltpu.VMEM((2, 16, *half), F32),
            pltpu.VMEM((2, 4, *half), F32),
            pltpu.VMEM((2, 4, *half), F32),
            pltpu.VMEM((2, 4, *half), F32),
            pltpu.VMEM((2, 4, *half), F32),
            pltpu.VMEM((2, *half), F32),
            pltpu.VMEM((2, *half), F32),
            pltpu.VMEM((2, *half), F32),
            pltpu.VMEM((2, 8, 8, 640), F32),
            pltpu.VMEM((2, 8, 8, 640), F32),
            pltpu.VMEM((2, 8, 8, 640), F32),
            dma((3,)),
            dma((2,)),
            dma((2,)),
            dma((2,)),
            dma((2, 16)),
            dma((2,)),
            dma((2,)),
            dma((2, 16)),
            dma((2,)),
            dma((2, 4)),
            dma((2, 4)),
            dma((2, 4)),
            dma((2,)),
            dma((2,)),
            dma((2,)),
            dma((2,)),
            dma((2,)),
            dma((2,)),
            dma((2,)),
            dma((2,)),
        ],
        compiler_params=pltpu.CompilerParams(collective_id=0, has_side_effects=True, vmem_limit_bytes=62 * 2**20),
    )(
        features, renoise, critic_grad, student_step, teacher_step, student_in, student_out.T, teacher_in, teacher_out.T,
        *vectors, selection(), membership(),
    )
    return grad_in, grad_out_t.T, grad_gain[0], grad_shift[0]


def solution(mesh):
    return jax.shard_map(
        local,
        mesh=mesh,
        in_specs=(
            P("dp", None, None),
            P("dp", None, None),
            P("dp", None, None),
            P("dp"),
            P("dp"),
            P("dp", None),
            P("dp"),
            P("dp"),
            P(None, "dp"),
            P("dp", None),
            P("dp"),
            P("dp"),
            P(None, "dp"),
        ),
        out_specs=(P("dp", None), P(None, "dp"), P("dp"), P("dp")),
        check_vma=False,
    )
```

```python
import functools
import math

import jax
import jax.numpy as jnp
import numpy as np
from jax import lax
from jax.experimental import pallas as pl
from jax.experimental.pallas import tpu as pltpu
from jax.sharding import PartitionSpec as P

GROUPS = 32
STEPS_T = 1000
EPS = 1e-05
MESH = pl.DeviceIdType.MESH
F32 = jnp.float32
BF16 = jnp.bfloat16


def dev(y, z, x, c):
    return ((y * 8 + z) * 4 + x) * 2 + c


def where_am_i():
    me = lax.axis_index("dp")
    c = lax.rem(me, 2)
    x = lax.rem(lax.div(me, 2), 4)
    z = lax.rem(lax.div(me, 8), 8)
    y = lax.div(me, 64)
    return y, z, x, c


class Ring:
    def __init__(self, b, y, z, x, c):
        r = lax.rem(c + b, 2)
        self.r = r
        self.p = (1 - r) * y + r * x
        self.q = (1 - r) * x + r * y
        self.at = (y, z, x, c)

    def block(self, dp, dq):
        pp = lax.rem(self.p + dp, 4)
        qq = lax.rem(self.q + dq, 4)
        return pp * (4 - 3 * self.r) + qq * (1 + 3 * self.r)

    def first(self, d):
        y, z, x, c = self.at
        r = self.r
        return dev(lax.rem(y + (1 - r) * d, 4), z, lax.rem(x + r * d, 4), c)

    def second(self, d):
        y, z, x, c = self.at
        r = self.r
        return dev(lax.rem(y + r * d, 4), z, lax.rem(x + (1 - r) * d, 4), c)


def signal(device):
    pl.semaphore_signal(pltpu.get_barrier_semaphore(), inc=1, device_id=(device,), device_id_type=MESH)


def remote(src, dst, ssem, rsem, device):
    return pltpu.make_async_remote_copy(
        src_ref=src, dst_ref=dst, send_sem=ssem, recv_sem=rsem, device_id=(device,), device_id_type=MESH
    )


def greet_planes(y, z, x, c):
    for d in (1, 2, 3):
        signal(dev(y, z, lax.rem(x + d, 4), c))
        signal(dev(lax.rem(y + d, 4), z, x, c))
    signal(dev(y, z, x, 1 - c))


ROWS = 256
STEPS = 4


def plan_of(step):
    index = lax.broadcasted_iota(jnp.int32, (8, 128), 0) * 128 + lax.broadcasted_iota(jnp.int32, (8, 128), 1)
    lo = math.sqrt(0.00085)
    hi = math.sqrt(0.012)
    betas = (lo + (hi - lo) * index.astype(F32) / (STEPS_T - 1)) ** 2
    logs = jnp.where(index <= step, jnp.log(1.0 - betas), 0.0)
    return jnp.exp(jnp.sum(jnp.sum(logs, axis=1, keepdims=True), axis=0, keepdims=True))


def embed(tval, width):
    half = width // 2
    lane = lax.broadcasted_iota(jnp.int32, (8, width), 1)
    index = jnp.where(lane < half, lane, lane - half).astype(F32)
    angles = tval * jnp.exp(-math.log(10000.0) * index / half)
    return jnp.where(lane < half, jnp.cos(angles), jnp.sin(angles))


def by_parts(value, indicator, dims):
    total = None
    for _ in range(3):
        part = value.astype(BF16)
        value = value - part.astype(F32)
        term = lax.dot_general(part, indicator, (dims, ((), ())), preferred_element_type=F32)
        total = term if total is None else total + term
    return total


def per_group(sums, indicator, count):
    groups = by_parts(sums, indicator, ((1,), (0,)))
    return jnp.broadcast_to(jnp.sum(groups, axis=0, keepdims=True), groups.shape) / count


def per_channel(groups, indicator):
    return by_parts(groups, indicator, ((1,), (1,)))


def eights(value):
    return jnp.sum(value.reshape(value.shape[0] // 8, 8, value.shape[1]), axis=0)


def kernel(
    feat_hbm, noise_hbm, critic_hbm, s_step, t_step, si_ref, so_ref, ti_ref, to_ref, sg_ref, ss_ref, tg_ref, ts_ref, sel_ref, ind_ref,
    in_ref, out_ref, gain_ref, shift_ref,
    feat, noise, critic, vecs, rawf, raw, rbuf, wb, w, vec, hid, pre, act, sample, dpre, sums, stat, emb,
    grad, sib, t1, fm, fp, acc, u1, um, up, stage, mid, fin,
    l_sem, r_send, r_recv, s_send, s_recv, s_sib,
    h_send, h_recv, q_send, t_recv, m_recv, p_recv, p_send, ut_recv, um_recv, up_recv, e_send, e_recv, f_send, f_recv,
):
    y, z, x, c = where_am_i()
    mine = lax.div(z, 2) == x
    loads = [
        pltpu.make_async_copy(src.at[0], dst, l_sem.at[n])
        for n, (src, dst) in enumerate(((feat_hbm, feat), (noise_hbm, noise), (critic_hbm, critic)))
    ]
    loads[0].start()

    greet_planes(y, z, x, c)
    for k in range(1, 16):
        signal(dev(y, 2 * x + lax.rem(z + k // 8, 2), lax.rem(x + k // 2, 4), lax.rem(c + k, 2)))

    @pl.when(jnp.logical_not(mine))
    def _():
        signal(dev(y, 2 * x + lax.rem(z, 2), x, c))

    for d in (1, 2, 3):
        signal(dev(y, z, lax.rem(x + d, 4), 1 - c))
    for k in range(1, 8):
        signal(dev(y, lax.rem(z + k, 8), x, c))

    rawf[...] = jnp.zeros_like(rawf)
    place = 5 * lax.rem(lax.axis_index("dp"), 16)
    vecs[...] = jnp.zeros_like(vecs)
    for n, ref in enumerate((sg_ref, ss_ref, tg_ref, ts_ref)):
        vecs[n : n + 1, 0:5] = ref[...].astype(F32)
    spread = pltpu.roll(vecs[...], place, 1)
    for core, pair in enumerate(((si_ref, ti_ref), (so_ref, to_ref))):
        for b, ref in enumerate(pair):
            shard = ref[...].astype(F32)
            for j in range(5):
                r = 16 * (2 * b + j // 3) + 5 * (j % 3)
                rawf[core, r : r + 5, :] = shard[:, 128 * j : 128 * j + 128]
            for h in range(2):
                r = 16 * (2 * b + h) + 15
                rawf[core, r : r + 1, :] = spread[2 * b + h : 2 * b + h + 1]
    raw[...] = rawf[...].astype(BF16)
    loads[0].wait()
    loads[1].start()
    loads[2].start()

    def rows_of(i):
        return pl.ds(pl.multiple_of(i * ROWS, ROWS), ROWS)

    sums[...] = jnp.zeros_like(sums)

    @pl.loop(0, STEPS)
    def _(i):
        sums[0] += eights(feat[rows_of(i), :].astype(F32))

    pl.semaphore_wait(pltpu.get_barrier_semaphore(), jnp.where(mine, 32, 33))

    slot = lax.rem(z, 2) * 8 + x * 2 + c
    to_x = lax.div(z, 2)
    for b in range(2):

        def shard(cc):
            return raw.at[cc, pl.ds(32 * b, 32)]

        for k in range(1, 16):
            cc = lax.rem(c + k, 2)
            remote(
                shard(cc), rbuf.at[b, slot], r_send.at[b], r_recv.at[b], dev(y, lax.rem(z + k // 2, 8), to_x, cc)
            ).start()
        own = pltpu.make_async_copy(shard(c), rbuf.at[b, slot], r_recv.at[b])
        first = remote(shard(c), rbuf.at[b, slot], r_send.at[b], r_recv.at[b], dev(y, z, to_x, c))

        @pl.when(mine)
        def _():
            own.start()

        @pl.when(jnp.logical_not(mine))
        def _():
            first.start()

    count = 40 * 1024

    def mean_to(b):
        stat[b, 0:8, :] = per_channel(per_group(sums[0], ind_ref[...], count), ind_ref[...])

    def scale_to(b):
        var = per_group(sums[1], ind_ref[...], count)
        stat[b, 8:16, :] = per_channel(lax.rsqrt(var + EPS), ind_ref[...])

    mean_to(0)

    @pl.loop(0, STEPS)
    def _(i):
        off = feat[rows_of(i), :].astype(F32) - stat[0, 0:1, :]
        sums[1] += eights(off * off)

    scale_to(0)
    emb[0] = embed((999 - 250 * s_step[0]).astype(F32), 640)
    emb[1] = embed(t_step[0].astype(F32), 640)

    rings = [Ring(b, y, z, x, c) for b in range(2)]

    def at(b, g):
        return wb.at[(b * 2 + c) * 16 + g]

    def send(b, g, device):
        remote(at(b, g), at(b, g), s_send.at[b], s_recv.at[b, g], device).start()

    def hand(b, g):
        remote(at(b, g), at(b, g), s_send.at[b], s_sib.at[b], dev(y, z, x, 1 - c)).start()

    def wait(b, g):
        remote(at(b, g), at(b, g), s_send.at[b], s_recv.at[b, g], dev(y, z, x, 1 - c)).wait_recv()

    row = lax.broadcasted_iota(jnp.int32, (16, 128), 0)
    def own_block(b):
        ring = rings[b]
        g = ring.block(0, 0)
        k = (b * 2 + c) * 16 + g
        pltpu.make_async_copy(rbuf.at[b], rbuf.at[b], r_recv.at[b]).wait()
        outs = []
        for h in range(2):
            tile = rbuf[b, :, 16 * h : 16 * h + 16, :].reshape(256, 128)
            out = jnp.dot(sel_ref[...], tile, preferred_element_type=F32)
            outs.append(out[240:256])
            for i in range(3):
                j = 3 * h + i
                if j < 5:
                    wb[k, 80 * j : 80 * j + 80, :] = out[80 * i : 80 * i + 80].astype(BF16)
        wb[k, 400:416, :] = jnp.where(row == 0, outs[0], outs[1]).astype(BF16)
        send(b, g, ring.first(1))
        send(b, g, ring.first(3))
        send(b, g, ring.first(2))
        send(b, g, ring.second(1))
        send(b, g, ring.second(3))
        hand(b, g)

    def gather_first(b):
        ring = rings[b]
        for d in (3, 1, 2):
            g = ring.block(d, 0)
            wait(b, g)
            send(b, g, ring.second(1))
            send(b, g, ring.second(3))
            hand(b, g)

    def gather_second(b, m):
        ring = rings[b]
        n = m % 4
        on = 3 if n % 2 == 0 else 1
        g = ring.block((0, 3, 1, 2)[n], on if m < 4 else 4 - on)
        wait(b, g)
        if m < 4:
            send(b, g, ring.second(4 - on))
        hand(b, g)

    def gather_last(b):
        for d in (0, 3, 1, 2):
            g = rings[b].block(d, 2)
            wait(b, g)
            hand(b, g)

    def gathered(b):
        pltpu.make_async_copy(wb.at[pl.ds(0, 16)], wb.at[pl.ds(0, 16)], s_sib.at[b]).wait()
        for n in (2 * b, 2 * b + 1):
            for j in range(5):
                w[n, :, 128 * j : 128 * j + 128] = wb[16 * n : 16 * n + 16, 80 * j : 80 * j + 80, :].reshape(1280, 128)
        lane = lax.broadcasted_iota(jnp.int32, (16, 128), 1)
        parts = [jnp.zeros((16, 128), F32) for _ in range(10)]
        for g in range(16):
            tile, s = divmod(80 * g, 128)
            v = wb[2 * b * 16 + g, 400:416, :].astype(F32)
            if s:
                v = pltpu.roll(v, s, 1)
            parts[tile] += jnp.where(lane >= s, v, 0.0)
            if s + 80 > 128:
                parts[tile + 1] += jnp.where(lane < s, v, 0.0)
        for n in range(10):
            vec[b, :, 128 * n : 128 * n + 128] = parts[n]

    own_block(0)
    own_block(1)
    gather_first(0)
    for m in range(4):
        gather_second(0, m)
    gather_first(1)
    for m in range(4, 8):
        gather_second(0, m)
    gather_last(0)
    gathered(0)

    keep = plan_of(t_step[0])
    root, other_root = jnp.sqrt(keep), jnp.sqrt(1.0 - keep)
    nt = (((1,), (1,)), ((), ()))
    sums[...] = jnp.zeros_like(sums)
    loads[1].wait()

    @pl.loop(0, STEPS)
    def _(i):
        s = rows_of(i)
        field = feat[s, :].astype(F32)
        normed = (field - stat[0, 0:1, :]) * stat[0, 8:9, :]
        hid[s, :] = (normed * vec[0, 0:1, :] + vec[0, 1:2, :]).astype(BF16)
        u = jnp.dot(hid[s, :], w[0], preferred_element_type=F32) + emb[0, 0:1, :]
        pre[s, :] = u
        act[s, :] = (u * jax.nn.sigmoid(u)).astype(BF16)
        for n in range(4):

            @pl.when(i == n)
            def _(n=n):
                gather_second(1, 2 * n)

        out = field + lax.dot_general(act[s, :], w[1], nt, preferred_element_type=F32)
        sample[s, :] = out
        noisy = (root * out + other_root * noise[s, :].astype(F32)).astype(BF16)
        noise[s, :] = noisy
        sums[0] += eights(noisy.astype(F32))
        for n in range(4):

            @pl.when(i == n)
            def _(n=n):
                gather_second(1, 2 * n + 1)

    gather_last(1)
    mean_to(1)

    @pl.loop(0, STEPS)
    def _(i):
        off = noise[rows_of(i), :].astype(F32) - stat[1, 0:1, :]
        sums[1] += eights(off * off)

    scale_to(1)
    gathered(1)
    loads[2].wait()

    norm = 1.0 / 512.0

    @pl.loop(0, STEPS)
    def _(i):
        s = rows_of(i)
        field = noise[s, :].astype(F32)
        normed = (field - stat[1, 0:1, :]) * stat[1, 8:9, :]
        h = (normed * vec[1, 0:1, :] + vec[1, 1:2, :]).astype(BF16)
        u = jnp.dot(h, w[2], preferred_element_type=F32) + emb[1, 0:1, :]
        a = (u * jax.nn.sigmoid(u)).astype(BF16)
        target = field + lax.dot_general(a, w[3], nt, preferred_element_type=F32)
        critic[s, :] = ((2.0 * keep * (sample[s, :] - target) + critic[s, :].astype(F32)) * norm).astype(BF16)

    def to_sibling(b, g):
        return remote(grad.at[b, g, 1 - c], sib.at[b, g], h_send.at[b], h_recv.at[b, g], dev(y, z, x, 1 - c))

    def term(b, left, right):
        for tile in range(2):
            out = lax.dot_general(
                left[:, 640 * tile : 640 * tile + 640], right[...], (((0,), (0,)), ((), ())), preferred_element_type=F32
            )
            for n in range(8):
                for h in range(2):
                    for j in range(5):
                        grad[b, 8 * tile + n, h, 40 * j : 40 * j + 40, :] = out[
                            80 * n + 40 * h : 80 * n + 40 * h + 40, 128 * j : 128 * j + 128
                        ]
            for n in range(8):
                to_sibling(b, 8 * tile + n).start()

    for g in range(16):
        for h in range(2):
            grad[0, g, h, 200:208, :] = jnp.zeros((8, 128), F32)
    term(0, critic, act)

    def meet(b, g, *more):
        to_sibling(b, g).wait_recv()
        total = sib[b, g] + grad[b, g, c]
        for ref in more:
            total += ref[...]
        return total

    def push(b, g, dst, recv, d):
        remote(sib.at[b, g], dst, q_send.at[b], recv, rings[b].second(d)).start()

    def reduce_far(b):
        for k in range(4):
            g = rings[b].block((2, 1, 3, 0)[k], 2)
            sib[b, g] = meet(b, g)
            push(b, g, t1.at[b, k], t_recv.at[b, k], 1 if k % 2 == 0 else 3)

    def reduce_direct(b):
        for k in range(4):
            e = 3 if k % 2 == 0 else 1
            g = rings[b].block((2, 1, 3, 0)[k], e)
            sib[b, g] = meet(b, g)
            if e == 1:
                push(b, g, fm.at[b, k], m_recv.at[b, k], 1)
            else:
                push(b, g, fp.at[b, k], p_recv.at[b, k], 3)

    def reduce_through(b):
        for k in range(4):
            e = 1 if k % 2 == 0 else 3
            g = rings[b].block((2, 1, 3, 0)[k], e)
            remote(t1.at[b, k], t1.at[b, k], q_send.at[b], t_recv.at[b, k], rings[b].second(1)).wait_recv()
            sib[b, g] = meet(b, g, t1.at[b, k])
            if e == 1:
                push(b, g, fm.at[b, k], m_recv.at[b, k], 1)
            else:
                push(b, g, fp.at[b, k], p_recv.at[b, k], 3)

    def arrive(b, dst, recv):
        remote(dst, dst, p_send.at[b], recv, rings[b].first(1)).wait_recv()

    def reduce_first(b, k):
        g = rings[b].block((2, 1, 3, 0)[k], 0)
        arrive(b, fm.at[b, k], m_recv.at[b, k])
        arrive(b, fp.at[b, k], p_recv.at[b, k])
        acc[b, k] = meet(b, g, fm.at[b, k], fp.at[b, k])
        if k < 3:
            dst, recv, d = ((u1, ut_recv, 2), (um, um_recv, 1), (up, up_recv, 3))[k]
            remote(acc.at[b, k], dst.at[b], p_send.at[b], recv.at[b], rings[b].first(d)).start()

    def pieces(b):
        arrive(b, um.at[b], um_recv.at[b])
        arrive(b, up.at[b], up_recv.at[b])
        arrive(b, u1.at[b], ut_recv.at[b])
        total = acc[b, 3] + um[b] + up[b] + u1[b]
        here = x * 2 + c
        for s in range(8):
            for j in range(5):
                stage[b, s, 0:5, 128 * j : 128 * j + 128] = total[40 * j + 5 * s : 40 * j + 5 * s + 5]
            v = total[200:208]
            if s:
                v = pltpu.roll(v, 128 - 5 * s, 1)
            stage[b, s, 5:7, 0:128] = v[0:2]

            @pl.when(here != s)
            def _(s=s):
                remote(
                    stage.at[b, s], mid.at[b, here], e_send.at[b], e_recv.at[b], dev(y, z, s // 2, s % 2)
                ).start()

            @pl.when(here == s)
            def _(s=s):
                pltpu.make_async_copy(stage.at[b, s], mid.at[b, here], e_recv.at[b]).start()

    def spread_pieces(b):
        pltpu.make_async_copy(mid.at[b], mid.at[b], e_recv.at[b]).wait()
        for k in (4, 3, 5, 2, 6, 1, 7):
            to = lax.rem(z + k, 8)
            remote(mid.at[b, to], fin.at[b, z], f_send.at[b], f_recv.at[b], dev(y, to, x, c)).start()
        pltpu.make_async_copy(mid.at[b, z], fin.at[b, z], f_recv.at[b]).start()

    sums[...] = jnp.zeros_like(sums)

    @pl.loop(0, STEPS)
    def _(i):
        s = rows_of(i)
        d_act = jnp.dot(critic[s, :], w[1], preferred_element_type=F32)
        u = pre[s, :]
        sig = jax.nn.sigmoid(u)
        dp = (d_act * sig * (1.0 + u * (1.0 - sig))).astype(BF16)
        dpre[s, :] = dp
        d_hid = lax.dot_general(dp, w[0], nt, preferred_element_type=F32)
        normed = (feat[s, :].astype(F32) - stat[0, 0:1, :]) * stat[0, 8:9, :]
        sums[0] += eights(d_hid * normed)
        sums[1] += eights(d_hid)

        @pl.when(i == 1)
        def _():
            reduce_far(0)

        @pl.when(i == 2)
        def _():
            reduce_direct(0)

        @pl.when(i == 3)
        def _():
            reduce_through(0)

    top = lax.broadcasted_iota(jnp.int32, (8, 128), 0) == 0
    lane8 = lax.broadcasted_iota(jnp.int32, (8, 128), 1)
    lines = []
    for n in range(10):
        gains = jnp.sum(sums[0, :, 128 * n : 128 * n + 128], axis=0, keepdims=True)
        shifts = jnp.sum(sums[1, :, 128 * n : 128 * n + 128], axis=0, keepdims=True)
        lines.append(jnp.where(top, gains, shifts))
    for n in range(32):
        tile, s = divmod(40 * n, 128)
        v = pltpu.roll(lines[tile], 128 - s, 1) if s else lines[tile]
        if s + 40 > 128:
            v = jnp.where(lane8 < 128 - s, v, pltpu.roll(lines[tile + 1], 128 - s, 1))
        grad[1, n // 2, n % 2, 200:208, :] = v
    term(1, hid, dpre)

    for k in range(4):
        reduce_first(0, k)
    reduce_far(1)
    reduce_direct(1)
    pieces(0)
    reduce_through(1)
    spread_pieces(0)
    for k in range(4):
        reduce_first(1, k)
    pieces(1)
    pltpu.make_async_copy(fin.at[0], fin.at[0], f_recv.at[0]).wait()
    out_ref[...] = jnp.sum(fin[0], axis=0)[0:5]
    spread_pieces(1)
    pltpu.make_async_copy(fin.at[1], fin.at[1], f_recv.at[1]).wait()
    total = jnp.sum(fin[1], axis=0)
    in_ref[...] = total[0:5]
    gain_ref[...] = total[5:6, 0:5]
    shift_ref[...] = total[6:7, 0:5]

    for b in range(2):

        @pl.when(mine)
        def _():
            pltpu.make_async_copy(rbuf.at[b, pl.ds(0, 15)], rbuf.at[b, pl.ds(0, 15)], r_send.at[b]).wait()

        @pl.when(jnp.logical_not(mine))
        def _():
            pltpu.make_async_copy(rbuf.at[b], rbuf.at[b], r_send.at[b]).wait()

        pltpu.make_async_copy(wb.at[pl.ds(0, 31)], wb.at[pl.ds(0, 31)], s_send.at[b]).wait()
        pltpu.make_async_copy(sib.at[b], sib.at[b], h_send.at[b]).wait()
        pltpu.make_async_copy(sib.at[b, pl.ds(0, 12)], sib.at[b, pl.ds(0, 12)], q_send.at[b]).wait()
        pltpu.make_async_copy(acc.at[b, pl.ds(0, 3)], acc.at[b, pl.ds(0, 3)], p_send.at[b]).wait()
        pltpu.make_async_copy(fin.at[b, pl.ds(0, 7)], fin.at[b, pl.ds(0, 7)], e_send.at[b]).wait()
        pltpu.make_async_copy(fin.at[b, pl.ds(0, 7)], fin.at[b, pl.ds(0, 7)], f_send.at[b]).wait()


def selection():
    sel = np.zeros((256, 256), np.float32)
    for m in range(240):
        i, q = divmod(m, 80)
        sel[m, 16 * (q // 5) + 5 * i + q % 5] = 1.0
    for d in range(16):
        sel[240:242, 16 * d + 15] = 1.0
    return jnp.asarray(sel, BF16)


def membership():
    ind = np.zeros((1280, 128), np.float32)
    ind[np.arange(1280), np.arange(1280) // 40] = 1.0
    return jnp.asarray(ind, BF16)


def local(
    features,
    renoise,
    critic_grad,
    student_step,
    teacher_step,
    student_in,
    student_gain,
    student_shift,
    student_out,
    teacher_in,
    teacher_gain,
    teacher_shift,
    teacher_out,
):
    vectors = [v[None, :] for v in (student_gain, student_shift, teacher_gain, teacher_shift)]
    vmem = pl.BlockSpec(memory_space=pltpu.VMEM)
    smem = pl.BlockSpec(memory_space=pltpu.SMEM)
    hbm = pl.BlockSpec(memory_space=pl.ANY)
    half = (208, 128)
    dma = pltpu.SemaphoreType.DMA
    grad_in, grad_out_t, grad_gain, grad_shift = pl.pallas_call(
        kernel,
        out_shape=[jax.ShapeDtypeStruct(shape, F32) for shape in ((5, 640), (5, 640), (1, 5), (1, 5))],
        in_specs=[hbm] * 3 + [smem] * 2 + [vmem] * 10,
        out_specs=[vmem] * 4,
        scratch_shapes=[
            pltpu.VMEM((1024, 1280), BF16),
            pltpu.VMEM((1024, 1280), BF16),
            pltpu.VMEM((1024, 1280), BF16),
            pltpu.VMEM((8, 128), F32),
            pltpu.VMEM((2, 64, 128), F32),
            pltpu.VMEM((2, 64, 128), BF16),
            pltpu.VMEM((2, 16, 32, 128), BF16),
            pltpu.VMEM((64, 416, 128), BF16),
            pltpu.VMEM((4, 1280, 640), BF16),
            pltpu.VMEM((2, 16, 1280), F32),
            pltpu.VMEM((1024, 1280), BF16),
            pltpu.VMEM((1024, 640), F32),
            pltpu.VMEM((1024, 640), BF16),
            pltpu.VMEM((1024, 1280), F32),
            pltpu.VMEM((1024, 640), BF16),
            pltpu.VMEM((2, 8, 1280), F32),
            pltpu.VMEM((2, 16, 1280), F32),
            pltpu.VMEM((2, 8, 640), F32),
            pltpu.VMEM((2, 16, 2, *half), F32),
            pltpu.VMEM((2, 16, *half), F32),
            pltpu.VMEM((2, 4, *half), F32),
            pltpu.VMEM((2, 4, *half), F32),
            pltpu.VMEM((2, 4, *half), F32),
            pltpu.VMEM((2, 4, *half), F32),
            pltpu.VMEM((2, *half), F32),
            pltpu.VMEM((2, *half), F32),
            pltpu.VMEM((2, *half), F32),
            pltpu.VMEM((2, 8, 8, 640), F32),
            pltpu.VMEM((2, 8, 8, 640), F32),
            pltpu.VMEM((2, 8, 8, 640), F32),
            dma((3,)),
            dma((2,)),
            dma((2,)),
            dma((2,)),
            dma((2, 16)),
            dma((2,)),
            dma((2,)),
            dma((2, 16)),
            dma((2,)),
            dma((2, 4)),
            dma((2, 4)),
            dma((2, 4)),
            dma((2,)),
            dma((2,)),
            dma((2,)),
            dma((2,)),
            dma((2,)),
            dma((2,)),
            dma((2,)),
            dma((2,)),
        ],
        compiler_params=pltpu.CompilerParams(collective_id=0, has_side_effects=True, vmem_limit_bytes=62 * 2**20),
    )(
        features, renoise, critic_grad, student_step, teacher_step, student_in, student_out.T, teacher_in, teacher_out.T,
        *vectors, selection(), membership(),
    )
    return grad_in, grad_out_t.T, grad_gain[0], grad_shift[0]


def solution(mesh):
    return jax.shard_map(
        local,
        mesh=mesh,
        in_specs=(
            P("dp", None, None),
            P("dp", None, None),
            P("dp", None, None),
            P("dp"),
            P("dp"),
            P("dp", None),
            P("dp"),
            P("dp"),
            P(None, "dp"),
            P("dp", None),
            P("dp"),
            P("dp"),
            P(None, "dp"),
        ),
        out_specs=(P("dp", None), P(None, "dp"), P("dp"), P("dp")),
        check_vma=False,
    )
```

```python
import functools
import math

import jax
import jax.numpy as jnp
import numpy as np
from jax import lax
from jax.experimental import pallas as pl
from jax.experimental.pallas import tpu as pltpu
from jax.sharding import PartitionSpec as P

GROUPS = 32
STEPS_T = 1000
EPS = 1e-05
MESH = pl.DeviceIdType.MESH
F32 = jnp.float32
BF16 = jnp.bfloat16


def dev(y, z, x, c):
    return ((y * 8 + z) * 4 + x) * 2 + c


def where_am_i():
    me = lax.axis_index("dp")
    c = lax.rem(me, 2)
    x = lax.rem(lax.div(me, 2), 4)
    z = lax.rem(lax.div(me, 8), 8)
    y = lax.div(me, 64)
    return y, z, x, c


class Ring:
    def __init__(self, b, y, z, x, c):
        r = lax.rem(c + b, 2)
        self.r = r
        self.p = (1 - r) * y + r * x
        self.q = (1 - r) * x + r * y
        self.at = (y, z, x, c)

    def block(self, dp, dq):
        pp = lax.rem(self.p + dp, 4)
        qq = lax.rem(self.q + dq, 4)
        return pp * (4 - 3 * self.r) + qq * (1 + 3 * self.r)

    def first(self, d):
        y, z, x, c = self.at
        r = self.r
        return dev(lax.rem(y + (1 - r) * d, 4), z, lax.rem(x + r * d, 4), c)

    def second(self, d):
        y, z, x, c = self.at
        r = self.r
        return dev(lax.rem(y + r * d, 4), z, lax.rem(x + (1 - r) * d, 4), c)


def signal(device):
    pl.semaphore_signal(pltpu.get_barrier_semaphore(), inc=1, device_id=(device,), device_id_type=MESH)


def remote(src, dst, ssem, rsem, device):
    return pltpu.make_async_remote_copy(
        src_ref=src, dst_ref=dst, send_sem=ssem, recv_sem=rsem, device_id=(device,), device_id_type=MESH
    )


def greet_planes(y, z, x, c):
    for d in (1, 2, 3):
        signal(dev(y, z, lax.rem(x + d, 4), c))
        signal(dev(lax.rem(y + d, 4), z, x, c))
    signal(dev(y, z, x, 1 - c))


ROWS = 256
STEPS = 4


def plan_of(step):
    index = lax.broadcasted_iota(jnp.int32, (8, 128), 0) * 128 + lax.broadcasted_iota(jnp.int32, (8, 128), 1)
    lo = math.sqrt(0.00085)
    hi = math.sqrt(0.012)
    betas = (lo + (hi - lo) * index.astype(F32) / (STEPS_T - 1)) ** 2
    logs = jnp.where(index <= step, jnp.log(1.0 - betas), 0.0)
    return jnp.exp(jnp.sum(jnp.sum(logs, axis=1, keepdims=True), axis=0, keepdims=True))


def embed(tval, width):
    half = width // 2
    lane = lax.broadcasted_iota(jnp.int32, (8, width), 1)
    index = jnp.where(lane < half, lane, lane - half).astype(F32)
    angles = tval * jnp.exp(-math.log(10000.0) * index / half)
    return jnp.where(lane < half, jnp.cos(angles), jnp.sin(angles))


def by_parts(value, indicator, dims):
    total = None
    for _ in range(3):
        part = value.astype(BF16)
        value = value - part.astype(F32)
        term = lax.dot_general(part, indicator, (dims, ((), ())), preferred_element_type=F32)
        total = term if total is None else total + term
    return total


def per_group(sums, indicator, count):
    groups = by_parts(sums, indicator, ((1,), (0,)))
    return jnp.broadcast_to(jnp.sum(groups, axis=0, keepdims=True), groups.shape) / count


def per_channel(groups, indicator):
    return by_parts(groups, indicator, ((1,), (1,)))


def eights(value):
    return jnp.sum(value.reshape(value.shape[0] // 8, 8, value.shape[1]), axis=0)


def kernel(
    feat_hbm, noise_hbm, critic_hbm, s_step, t_step, si_ref, so_ref, ti_ref, to_ref, sg_ref, ss_ref, tg_ref, ts_ref, sel_ref, ind_ref,
    in_ref, out_ref, gain_ref, shift_ref,
    feat, noise, critic, vecs, rawf, raw, rbuf, wb, w, vec, hid, pre, act, sample, dpre, sums, stat, emb,
    grad, sib, t1, fm, fp, acc, u1, um, up, stage, mid, fin,
    l_sem, r_send, r_recv, s_send, s_recv, s_sib,
    h_send, h_recv, q_send, t_recv, m_recv, p_recv, p_send, ut_recv, um_recv, up_recv, e_send, e_recv, f_send, f_recv,
):
    y, z, x, c = where_am_i()
    mine = lax.div(z, 2) == x
    loads = [
        pltpu.make_async_copy(src.at[0], dst, l_sem.at[n])
        for n, (src, dst) in enumerate(((feat_hbm, feat), (noise_hbm, noise), (critic_hbm, critic)))
    ]
    loads[0].start()

    for k in range(1, 16):
        signal(dev(y, 2 * x + lax.rem(z + k // 8, 2), lax.rem(x + k // 2, 4), lax.rem(c + k, 2)))

    @pl.when(jnp.logical_not(mine))
    def _():
        signal(dev(y, 2 * x + lax.rem(z, 2), x, c))

    greet_planes(y, z, x, c)
    for d in (1, 2, 3):
        signal(dev(y, z, lax.rem(x + d, 4), 1 - c))
    for k in range(1, 8):
        signal(dev(y, lax.rem(z + k, 8), x, c))

    rawf[...] = jnp.zeros_like(rawf)
    place = 5 * lax.rem(lax.axis_index("dp"), 16)
    vecs[...] = jnp.zeros_like(vecs)
    for n, ref in enumerate((sg_ref, ss_ref, tg_ref, ts_ref)):
        vecs[n : n + 1, 0:5] = ref[...].astype(F32)
    spread = pltpu.roll(vecs[...], place, 1)
    for core, pair in enumerate(((si_ref, ti_ref), (so_ref, to_ref))):
        for b, ref in enumerate(pair):
            shard = ref[...].astype(F32)
            for j in range(5):
                r = 16 * (2 * b + j // 3) + 5 * (j % 3)
                rawf[core, r : r + 5, :] = shard[:, 128 * j : 128 * j + 128]
            for h in range(2):
                r = 16 * (2 * b + h) + 15
                rawf[core, r : r + 1, :] = spread[2 * b + h : 2 * b + h + 1]
    raw[...] = rawf[...].astype(BF16)
    loads[0].wait()
    loads[1].start()
    loads[2].start()

    def rows_of(i):
        return pl.ds(pl.multiple_of(i * ROWS, ROWS), ROWS)

    sums[...] = jnp.zeros_like(sums)

    @pl.loop(0, STEPS)
    def _(i):
        sums[0] += eights(feat[rows_of(i), :].astype(F32))

    pl.semaphore_wait(pltpu.get_barrier_semaphore(), jnp.where(mine, 32, 33))

    slot = lax.rem(z, 2) * 8 + x * 2 + c
    to_x = lax.div(z, 2)
    for b in range(2):

        def shard(cc):
            return raw.at[cc, pl.ds(32 * b, 32)]

        for k in (8, 9, 6, 7, 10, 11, 4, 5, 12, 13, 2, 3, 14, 15, 1):
            cc = lax.rem(c + k, 2)
            remote(
                shard(cc), rbuf.at[b, slot], r_send.at[b], r_recv.at[b], dev(y, lax.rem(z + k // 2, 8), to_x, cc)
            ).start()
        own = pltpu.make_async_copy(shard(c), rbuf.at[b, slot], r_recv.at[b])
        first = remote(shard(c), rbuf.at[b, slot], r_send.at[b], r_recv.at[b], dev(y, z, to_x, c))

        @pl.when(mine)
        def _():
            own.start()

        @pl.when(jnp.logical_not(mine))
        def _():
            first.start()

    count = 40 * 1024

    def mean_to(b):
        stat[b, 0:8, :] = per_channel(per_group(sums[0], ind_ref[...], count), ind_ref[...])

    def scale_to(b):
        var = per_group(sums[1], ind_ref[...], count)
        stat[b, 8:16, :] = per_channel(lax.rsqrt(var + EPS), ind_ref[...])

    mean_to(0)

    @pl.loop(0, STEPS)
    def _(i):
        off = feat[rows_of(i), :].astype(F32) - stat[0, 0:1, :]
        sums[1] += eights(off * off)

    scale_to(0)
    emb[0] = embed((999 - 250 * s_step[0]).astype(F32), 640)
    emb[1] = embed(t_step[0].astype(F32), 640)

    rings = [Ring(b, y, z, x, c) for b in range(2)]

    def at(b, g):
        return wb.at[(b * 2 + c) * 16 + g]

    def send(b, g, device):
        remote(at(b, g), at(b, g), s_send.at[b], s_recv.at[b, g], device).start()

    def hand(b, g):
        remote(at(b, g), at(b, g), s_send.at[b], s_sib.at[b], dev(y, z, x, 1 - c)).start()

    def wait(b, g):
        remote(at(b, g), at(b, g), s_send.at[b], s_recv.at[b, g], dev(y, z, x, 1 - c)).wait_recv()

    row = lax.broadcasted_iota(jnp.int32, (16, 128), 0)
    def own_block(b):
        ring = rings[b]
        g = ring.block(0, 0)
        k = (b * 2 + c) * 16 + g
        pltpu.make_async_copy(rbuf.at[b], rbuf.at[b], r_recv.at[b]).wait()
        outs = []
        for h in range(2):
            tile = rbuf[b, :, 16 * h : 16 * h + 16, :].reshape(256, 128)
            out = jnp.dot(sel_ref[...], tile, preferred_element_type=F32)
            outs.append(out[240:256])
            for i in range(3):
                j = 3 * h + i
                if j < 5:
                    wb[k, 80 * j : 80 * j + 80, :] = out[80 * i : 80 * i + 80].astype(BF16)
        wb[k, 400:416, :] = jnp.where(row == 0, outs[0], outs[1]).astype(BF16)
        send(b, g, ring.first(1))
        send(b, g, ring.first(3))
        send(b, g, ring.first(2))
        send(b, g, ring.second(1))
        send(b, g, ring.second(3))
        hand(b, g)

    def gather_first(b):
        ring = rings[b]
        for d in (3, 1, 2):
            g = ring.block(d, 0)
            wait(b, g)
            send(b, g, ring.second(1))
            send(b, g, ring.second(3))
            hand(b, g)

    def gather_second(b, m):
        ring = rings[b]
        n = m % 4
        on = 3 if n % 2 == 0 else 1
        g = ring.block((0, 3, 1, 2)[n], on if m < 4 else 4 - on)
        wait(b, g)
        if m < 4:
            send(b, g, ring.second(4 - on))
        hand(b, g)

    def gather_last(b):
        for d in (0, 3, 1, 2):
            g = rings[b].block(d, 2)
            wait(b, g)
            hand(b, g)

    def gathered(b):
        pltpu.make_async_copy(wb.at[pl.ds(0, 16)], wb.at[pl.ds(0, 16)], s_sib.at[b]).wait()
        for n in (2 * b, 2 * b + 1):
            for j in range(5):
                w[n, :, 128 * j : 128 * j + 128] = wb[16 * n : 16 * n + 16, 80 * j : 80 * j + 80, :].reshape(1280, 128)
        lane = lax.broadcasted_iota(jnp.int32, (16, 128), 1)
        parts = [jnp.zeros((16, 128), F32) for _ in range(10)]
        for g in range(16):
            tile, s = divmod(80 * g, 128)
            v = wb[2 * b * 16 + g, 400:416, :].astype(F32)
            if s:
                v = pltpu.roll(v, s, 1)
            parts[tile] += jnp.where(lane >= s, v, 0.0)
            if s + 80 > 128:
                parts[tile + 1] += jnp.where(lane < s, v, 0.0)
        for n in range(10):
            vec[b, :, 128 * n : 128 * n + 128] = parts[n]

    own_block(0)
    own_block(1)
    gather_first(0)
    for m in range(4):
        gather_second(0, m)
    gather_first(1)
    for m in range(4, 8):
        gather_second(0, m)
    gather_last(0)
    gathered(0)

    keep = plan_of(t_step[0])
    root, other_root = jnp.sqrt(keep), jnp.sqrt(1.0 - keep)
    nt = (((1,), (1,)), ((), ()))
    sums[...] = jnp.zeros_like(sums)
    loads[1].wait()

    @pl.loop(0, STEPS)
    def _(i):
        s = rows_of(i)
        field = feat[s, :].astype(F32)
        normed = (field - stat[0, 0:1, :]) * stat[0, 8:9, :]
        hid[s, :] = (normed * vec[0, 0:1, :] + vec[0, 1:2, :]).astype(BF16)
        u = jnp.dot(hid[s, :], w[0], preferred_element_type=F32) + emb[0, 0:1, :]
        pre[s, :] = u
        act[s, :] = (u * jax.nn.sigmoid(u)).astype(BF16)
        for n in range(4):

            @pl.when(i == n)
            def _(n=n):
                gather_second(1, 2 * n)

        out = field + lax.dot_general(act[s, :], w[1], nt, preferred_element_type=F32)
        sample[s, :] = out
        noisy = (root * out + other_root * noise[s, :].astype(F32)).astype(BF16)
        noise[s, :] = noisy
        sums[0] += eights(noisy.astype(F32))
        for n in range(4):

            @pl.when(i == n)
            def _(n=n):
                gather_second(1, 2 * n + 1)

    gather_last(1)
    mean_to(1)

    @pl.loop(0, STEPS)
    def _(i):
        off = noise[rows_of(i), :].astype(F32) - stat[1, 0:1, :]
        sums[1] += eights(off * off)

    scale_to(1)
    gathered(1)
    loads[2].wait()

    norm = 1.0 / 512.0

    @pl.loop(0, STEPS)
    def _(i):
        s = rows_of(i)
        field = noise[s, :].astype(F32)
        normed = (field - stat[1, 0:1, :]) * stat[1, 8:9, :]
        h = (normed * vec[1, 0:1, :] + vec[1, 1:2, :]).astype(BF16)
        u = jnp.dot(h, w[2], preferred_element_type=F32) + emb[1, 0:1, :]
        a = (u * jax.nn.sigmoid(u)).astype(BF16)
        target = field + lax.dot_general(a, w[3], nt, preferred_element_type=F32)
        critic[s, :] = ((2.0 * keep * (sample[s, :] - target) + critic[s, :].astype(F32)) * norm).astype(BF16)

    def to_sibling(b, g):
        return remote(grad.at[b, g, 1 - c], sib.at[b, g], h_send.at[b], h_recv.at[b, g], dev(y, z, x, 1 - c))

    def term(b, left, right):
        for tile in range(2):
            out = lax.dot_general(
                left[:, 640 * tile : 640 * tile + 640], right[...], (((0,), (0,)), ((), ())), preferred_element_type=F32
            )
            for n in range(8):
                for h in range(2):
                    for j in range(5):
                        grad[b, 8 * tile + n, h, 40 * j : 40 * j + 40, :] = out[
                            80 * n + 40 * h : 80 * n + 40 * h + 40, 128 * j : 128 * j + 128
                        ]
            for n in range(8):
                to_sibling(b, 8 * tile + n).start()

    for g in range(16):
        for h in range(2):
            grad[0, g, h, 200:208, :] = jnp.zeros((8, 128), F32)
    term(0, critic, act)

    def meet(b, g, *more):
        to_sibling(b, g).wait_recv()
        total = sib[b, g] + grad[b, g, c]
        for ref in more:
            total += ref[...]
        return total

    def push(b, g, dst, recv, d):
        remote(sib.at[b, g], dst, q_send.at[b], recv, rings[b].second(d)).start()

    def reduce_far(b):
        for k in range(4):
            g = rings[b].block((2, 1, 3, 0)[k], 2)
            sib[b, g] = meet(b, g)
            push(b, g, t1.at[b, k], t_recv.at[b, k], 1 if k % 2 == 0 else 3)

    def reduce_direct(b):
        for k in range(4):
            e = 3 if k % 2 == 0 else 1
            g = rings[b].block((2, 1, 3, 0)[k], e)
            sib[b, g] = meet(b, g)
            if e == 1:
                push(b, g, fm.at[b, k], m_recv.at[b, k], 1)
            else:
                push(b, g, fp.at[b, k], p_recv.at[b, k], 3)

    def reduce_through(b):
        for k in range(4):
            e = 1 if k % 2 == 0 else 3
            g = rings[b].block((2, 1, 3, 0)[k], e)
            remote(t1.at[b, k], t1.at[b, k], q_send.at[b], t_recv.at[b, k], rings[b].second(1)).wait_recv()
            sib[b, g] = meet(b, g, t1.at[b, k])
            if e == 1:
                push(b, g, fm.at[b, k], m_recv.at[b, k], 1)
            else:
                push(b, g, fp.at[b, k], p_recv.at[b, k], 3)

    def arrive(b, dst, recv):
        remote(dst, dst, p_send.at[b], recv, rings[b].first(1)).wait_recv()

    def reduce_first(b, k):
        g = rings[b].block((2, 1, 3, 0)[k], 0)
        arrive(b, fm.at[b, k], m_recv.at[b, k])
        arrive(b, fp.at[b, k], p_recv.at[b, k])
        acc[b, k] = meet(b, g, fm.at[b, k], fp.at[b, k])
        if k < 3:
            dst, recv, d = ((u1, ut_recv, 2), (um, um_recv, 1), (up, up_recv, 3))[k]
            remote(acc.at[b, k], dst.at[b], p_send.at[b], recv.at[b], rings[b].first(d)).start()

    def pieces(b):
        arrive(b, um.at[b], um_recv.at[b])
        arrive(b, up.at[b], up_recv.at[b])
        arrive(b, u1.at[b], ut_recv.at[b])
        total = acc[b, 3] + um[b] + up[b] + u1[b]
        here = x * 2 + c
        for s in range(8):
            for j in range(5):
                stage[b, s, 0:5, 128 * j : 128 * j + 128] = total[40 * j + 5 * s : 40 * j + 5 * s + 5]
            v = total[200:208]
            if s:
                v = pltpu.roll(v, 128 - 5 * s, 1)
            stage[b, s, 5:7, 0:128] = v[0:2]

            @pl.when(here != s)
            def _(s=s):
                remote(
                    stage.at[b, s], mid.at[b, here], e_send.at[b], e_recv.at[b], dev(y, z, s // 2, s % 2)
                ).start()

            @pl.when(here == s)
            def _(s=s):
                pltpu.make_async_copy(stage.at[b, s], mid.at[b, here], e_recv.at[b]).start()

    def spread_pieces(b):
        pltpu.make_async_copy(mid.at[b], mid.at[b], e_recv.at[b]).wait()
        for k in (4, 3, 5, 2, 6, 1, 7):
            to = lax.rem(z + k, 8)
            remote(mid.at[b, to], fin.at[b, z], f_send.at[b], f_recv.at[b], dev(y, to, x, c)).start()
        pltpu.make_async_copy(mid.at[b, z], fin.at[b, z], f_recv.at[b]).start()

    sums[...] = jnp.zeros_like(sums)

    @pl.loop(0, STEPS)
    def _(i):
        s = rows_of(i)
        d_act = jnp.dot(critic[s, :], w[1], preferred_element_type=F32)
        u = pre[s, :]
        sig = jax.nn.sigmoid(u)
        dp = (d_act * sig * (1.0 + u * (1.0 - sig))).astype(BF16)
        dpre[s, :] = dp
        d_hid = lax.dot_general(dp, w[0], nt, preferred_element_type=F32)
        normed = (feat[s, :].astype(F32) - stat[0, 0:1, :]) * stat[0, 8:9, :]
        sums[0] += eights(d_hid * normed)
        sums[1] += eights(d_hid)

        @pl.when(i == 1)
        def _():
            reduce_far(0)

        @pl.when(i == 2)
        def _():
            reduce_direct(0)

        @pl.when(i == 3)
        def _():
            reduce_through(0)

    top = lax.broadcasted_iota(jnp.int32, (8, 128), 0) == 0
    lane8 = lax.broadcasted_iota(jnp.int32, (8, 128), 1)
    lines = []
    for n in range(10):
        gains = jnp.sum(sums[0, :, 128 * n : 128 * n + 128], axis=0, keepdims=True)
        shifts = jnp.sum(sums[1, :, 128 * n : 128 * n + 128], axis=0, keepdims=True)
        lines.append(jnp.where(top, gains, shifts))
    for n in range(32):
        tile, s = divmod(40 * n, 128)
        v = pltpu.roll(lines[tile], 128 - s, 1) if s else lines[tile]
        if s + 40 > 128:
            v = jnp.where(lane8 < 128 - s, v, pltpu.roll(lines[tile + 1], 128 - s, 1))
        grad[1, n // 2, n % 2, 200:208, :] = v
    term(1, hid, dpre)

    for k in range(4):
        reduce_first(0, k)
    reduce_far(1)
    reduce_direct(1)
    pieces(0)
    reduce_through(1)
    spread_pieces(0)
    for k in range(4):
        reduce_first(1, k)
    pieces(1)
    pltpu.make_async_copy(fin.at[0], fin.at[0], f_recv.at[0]).wait()
    out_ref[...] = jnp.sum(fin[0], axis=0)[0:5]
    spread_pieces(1)
    pltpu.make_async_copy(fin.at[1], fin.at[1], f_recv.at[1]).wait()
    total = jnp.sum(fin[1], axis=0)
    in_ref[...] = total[0:5]
    gain_ref[...] = total[5:6, 0:5]
    shift_ref[...] = total[6:7, 0:5]

    for b in range(2):

        @pl.when(mine)
        def _():
            pltpu.make_async_copy(rbuf.at[b, pl.ds(0, 15)], rbuf.at[b, pl.ds(0, 15)], r_send.at[b]).wait()

        @pl.when(jnp.logical_not(mine))
        def _():
            pltpu.make_async_copy(rbuf.at[b], rbuf.at[b], r_send.at[b]).wait()

        pltpu.make_async_copy(wb.at[pl.ds(0, 31)], wb.at[pl.ds(0, 31)], s_send.at[b]).wait()
        pltpu.make_async_copy(sib.at[b], sib.at[b], h_send.at[b]).wait()
        pltpu.make_async_copy(sib.at[b, pl.ds(0, 12)], sib.at[b, pl.ds(0, 12)], q_send.at[b]).wait()
        pltpu.make_async_copy(acc.at[b, pl.ds(0, 3)], acc.at[b, pl.ds(0, 3)], p_send.at[b]).wait()
        pltpu.make_async_copy(fin.at[b, pl.ds(0, 7)], fin.at[b, pl.ds(0, 7)], e_send.at[b]).wait()
        pltpu.make_async_copy(fin.at[b, pl.ds(0, 7)], fin.at[b, pl.ds(0, 7)], f_send.at[b]).wait()


def selection():
    sel = np.zeros((256, 256), np.float32)
    for m in range(240):
        i, q = divmod(m, 80)
        sel[m, 16 * (q // 5) + 5 * i + q % 5] = 1.0
    for d in range(16):
        sel[240:242, 16 * d + 15] = 1.0
    return jnp.asarray(sel, BF16)


def membership():
    ind = np.zeros((1280, 128), np.float32)
    ind[np.arange(1280), np.arange(1280) // 40] = 1.0
    return jnp.asarray(ind, BF16)


def local(
    features,
    renoise,
    critic_grad,
    student_step,
    teacher_step,
    student_in,
    student_gain,
    student_shift,
    student_out,
    teacher_in,
    teacher_gain,
    teacher_shift,
    teacher_out,
):
    vectors = [v[None, :] for v in (student_gain, student_shift, teacher_gain, teacher_shift)]
    vmem = pl.BlockSpec(memory_space=pltpu.VMEM)
    smem = pl.BlockSpec(memory_space=pltpu.SMEM)
    hbm = pl.BlockSpec(memory_space=pl.ANY)
    half = (208, 128)
    dma = pltpu.SemaphoreType.DMA
    grad_in, grad_out_t, grad_gain, grad_shift = pl.pallas_call(
        kernel,
        out_shape=[jax.ShapeDtypeStruct(shape, F32) for shape in ((5, 640), (5, 640), (1, 5), (1, 5))],
        in_specs=[hbm] * 3 + [smem] * 2 + [vmem] * 10,
        out_specs=[vmem] * 4,
        scratch_shapes=[
            pltpu.VMEM((1024, 1280), BF16),
            pltpu.VMEM((1024, 1280), BF16),
            pltpu.VMEM((1024, 1280), BF16),
            pltpu.VMEM((8, 128), F32),
            pltpu.VMEM((2, 64, 128), F32),
            pltpu.VMEM((2, 64, 128), BF16),
            pltpu.VMEM((2, 16, 32, 128), BF16),
            pltpu.VMEM((64, 416, 128), BF16),
            pltpu.VMEM((4, 1280, 640), BF16),
            pltpu.VMEM((2, 16, 1280), F32),
            pltpu.VMEM((1024, 1280), BF16),
            pltpu.VMEM((1024, 640), F32),
            pltpu.VMEM((1024, 640), BF16),
            pltpu.VMEM((1024, 1280), F32),
            pltpu.VMEM((1024, 640), BF16),
            pltpu.VMEM((2, 8, 1280), F32),
            pltpu.VMEM((2, 16, 1280), F32),
            pltpu.VMEM((2, 8, 640), F32),
            pltpu.VMEM((2, 16, 2, *half), F32),
            pltpu.VMEM((2, 16, *half), F32),
            pltpu.VMEM((2, 4, *half), F32),
            pltpu.VMEM((2, 4, *half), F32),
            pltpu.VMEM((2, 4, *half), F32),
            pltpu.VMEM((2, 4, *half), F32),
            pltpu.VMEM((2, *half), F32),
            pltpu.VMEM((2, *half), F32),
            pltpu.VMEM((2, *half), F32),
            pltpu.VMEM((2, 8, 8, 640), F32),
            pltpu.VMEM((2, 8, 8, 640), F32),
            pltpu.VMEM((2, 8, 8, 640), F32),
            dma((3,)),
            dma((2,)),
            dma((2,)),
            dma((2,)),
            dma((2, 16)),
            dma((2,)),
            dma((2,)),
            dma((2, 16)),
            dma((2,)),
            dma((2, 4)),
            dma((2, 4)),
            dma((2, 4)),
            dma((2,)),
            dma((2,)),
            dma((2,)),
            dma((2,)),
            dma((2,)),
            dma((2,)),
            dma((2,)),
            dma((2,)),
        ],
        compiler_params=pltpu.CompilerParams(collective_id=0, has_side_effects=True, vmem_limit_bytes=62 * 2**20),
    )(
        features, renoise, critic_grad, student_step, teacher_step, student_in, student_out.T, teacher_in, teacher_out.T,
        *vectors, selection(), membership(),
    )
    return grad_in, grad_out_t.T, grad_gain[0], grad_shift[0]


def solution(mesh):
    return jax.shard_map(
        local,
        mesh=mesh,
        in_specs=(
            P("dp", None, None),
            P("dp", None, None),
            P("dp", None, None),
            P("dp"),
            P("dp"),
            P("dp", None),
            P("dp"),
            P("dp"),
            P(None, "dp"),
            P("dp", None),
            P("dp"),
            P("dp"),
            P(None, "dp"),
        ),
        out_specs=(P("dp", None), P(None, "dp"), P("dp"), P("dp")),
        check_vma=False,
    )
```
